128 devices in a mesh: seq: 16 (over z, x_hi, core), head: 8 (over y, x_lo).
Axes of the slice: x: 4 (x_hi: 2, x_lo: 2; x = x_hi * 2 + x_lo), y: 4, z: 4, core: 2. Of those that a mesh axis runs over, the one named last changes fastest.
Arguments:
- residual: bfloat16 [128, 4, 32, 4096], P('head', None, 'seq'), may hold values from -6 to 6
- spatial_query: bfloat16 [128, 4, 32, 4096], P(None, None, 'seq', 'head'), may hold values from -6 to 6
- spatial_key: bfloat16 [128, 4, 32, 4096], P(None, None, 'seq', 'head'), may hold values from -6 to 6
- spatial_value: bfloat16 [128, 4, 32, 4096], P(None, None, 'seq', 'head'), may hold values from -6 to 6
- spatial_out: bfloat16 [4096, 4096], P('head', 'seq'), may hold values from -0.09375 to 0.09375
- temporal_query: bfloat16 [4096, 4096], P('seq', 'head'), may hold values from -0.09375 to 0.09375
- temporal_key: bfloat16 [4096, 4096], P('seq', 'head'), may hold values from -0.09375 to 0.09375
- temporal_value: bfloat16 [4096, 4096], P('seq', 'head'), may hold values from -0.09375 to 0.09375
- temporal_out: bfloat16 [4096, 4096], P('head', 'seq'), may hold values from -0.09375 to 0.09375
Outputs:
- video_out: bfloat16 [128, 4, 32, 4096], P('head', None, 'seq')
The draws below stay inside these ranges and needn't reach their ends.
All inputs are finite; a program needn't handle non-finite values.
Results may differ from the reference program's by a relative error of at most 0.014.
Values may be sent and summed in bfloat16 or wider, within the bound.
No kernel may reach another device: no remote copies, remote signals or barrier semaphores. Data moves between devices by JAX's collectives and lax.ppermute only.
A program may use at most 128 MiB of HBM per device.

```python
import jax
import jax.numpy as jnp
from jax import lax

D = 4096
HDIM = 128
P_SIZE = 128
FRAMES = 32
VIDEOS = 4
N_HEAD = 8


def level_of(rng, extent, split, least, top_value):
    level = 1.0
    for axis_at, parts in split:
        steps = jax.random.uniform(jax.random.fold_in(jax.random.fold_in(rng, 6), axis_at), (parts,), jnp.float32, least / len(split), top_value / len(split))
        level = level * jnp.repeat(jnp.exp(steps), extent[axis_at] // parts).reshape((-1,) + (1,) * (len(extent) - 1 - axis_at))
    return level


def noise(key, shape, scale, reach, pieces=(), dtype=jnp.bfloat16):
    array = scale * jax.random.normal(key, shape, jnp.float32)
    if pieces:
        array = array * level_of(key, shape, pieces, -0.22, 0.18)
    return jnp.clip(array, -reach, reach).astype(dtype)


def setup_inputs(seed: int = 0) -> dict:
    key_list = jax.random.split(jax.random.key(seed), 10)
    return {
        "residual": noise(key_list[0], (P_SIZE, VIDEOS, FRAMES, D), 1.0, 6.0, ((0, 8), (2, 16))),
        "spatial_query": noise(key_list[1], (P_SIZE, VIDEOS, FRAMES, D), 1.0, 6.0, ((2, 16), (3, 8))),
        "spatial_key": noise(key_list[2], (P_SIZE, VIDEOS, FRAMES, D), 1.0, 6.0, ((2, 16), (3, 8))),
        "spatial_value": noise(key_list[3], (P_SIZE, VIDEOS, FRAMES, D), 1.0, 6.0, ((2, 16), (3, 8))),
        "spatial_out": noise(key_list[4], (D, D), D ** -0.5, 0.09375, ((0, 8), (1, 16))),
        "temporal_query": noise(key_list[5], (D, D), D ** -0.5, 0.09375, ((0, 16), (1, 8))),
        "temporal_key": noise(key_list[6], (D, D), D ** -0.5, 0.09375, ((0, 16), (1, 8))),
        "temporal_value": noise(key_list[7], (D, D), D ** -0.5, 0.09375, ((0, 16), (1, 8))),
        "temporal_out": noise(key_list[8], (D, D), D ** -0.5, 0.09375, ((0, 8), (1, 16))),
    }


def attend(queries, keys_in, values_in, seq_first):
    head_total = queries.shape[-1] // HDIM
    shaped = [member.reshape(member.shape[:2] + (head_total, HDIM)).astype(jnp.float32) for member in (queries, keys_in, values_in)]
    if seq_first:
        patterns = ('ighc,jghc->ghij', 'ghij,jghc->ighc')
    else:
        patterns = ('gihc,gjhc->ghij', 'ghij,gjhc->gihc')
    scores = jnp.einsum(patterns[0], shaped[0], shaped[1]) * HDIM ** (-0.5)
    exponent = jnp.exp(scores)
    weights = (exponent / lax.optimization_barrier(jnp.sum(exponent, axis=-1, keepdims=True))).astype(jnp.bfloat16)
    context = jnp.einsum(patterns[1], weights.astype(jnp.float32), shaped[2])
    return context.astype(jnp.bfloat16).reshape(queries.shape)

def head_sum(context, weight):
    group_size = context.shape[1] // N_HEAD
    running = jnp.zeros((context.shape[0], weight.shape[1]), jnp.float32)
    for group_index in range(N_HEAD):
        lower = group_index * group_size
        partial_term = jnp.dot(context[:, lower:lower + group_size], weight[lower:lower + group_size], preferred_element_type=jnp.float32)
        running = running + lax.optimization_barrier(partial_term.astype(jnp.bfloat16)).astype(jnp.float32)
    return running

def layer_norm(values_in):
    values_f = values_in.astype(jnp.float32)
    centred = values_f - lax.optimization_barrier(jnp.mean(values_f, axis=-1, keepdims=True))
    variance = lax.optimization_barrier(jnp.mean(centred * centred, axis=-1, keepdims=True))
    return (centred * lax.rsqrt(variance + 1e-06)).astype(jnp.bfloat16)

def reference(residual, spatial_query, spatial_key, spatial_value, spatial_out, temporal_query, temporal_key, temporal_value, temporal_out):
    layout = (P_SIZE, VIDEOS * FRAMES, D)
    spatial_context = attend(spatial_query.reshape(layout), spatial_key.reshape(layout), spatial_value.reshape(layout), True).reshape(-1, D)
    middle = (residual.reshape(-1, D).astype(jnp.float32) + head_sum(spatial_context, spatial_out)).astype(jnp.bfloat16)
    normed = layer_norm(middle)
    projected = [jnp.dot(normed, weight, preferred_element_type=jnp.float32).astype(jnp.bfloat16).reshape(P_SIZE * VIDEOS, FRAMES, D) for weight in (temporal_query, temporal_key, temporal_value)]
    temporal_context = attend(projected[0], projected[1], projected[2], False).reshape(-1, D)
    finished = (middle.astype(jnp.float32) + head_sum(temporal_context, temporal_out)).astype(jnp.bfloat16)
    return finished.reshape(P_SIZE, VIDEOS, FRAMES, D)
```

```python
import numpy as np

import jax
import jax.numpy as jnp
from jax import lax
from jax.experimental import pallas as pl
from jax.experimental.pallas import tpu as pltpu
from jax.sharding import Mesh
from jax.sharding import PartitionSpec as P

HDIM = 128
AXES = ("z", "xh", "c", "y", "xl")
SIZES = (4, 2, 2, 4, 2)
RING = 4
VMEM_LIMIT = 58 * 1024 * 1024


def permutation(move):
    pairs = []
    for source in range(int(np.prod(SIZES))):
        z, xh, c, y, xl = (int(v) for v in np.unravel_index(source, SIZES))
        z, x, c, y = (v % n for v, n in zip(move(z, 2 * xh + xl, c, y), (4, 4, 2, 4)))
        pairs.append((source, int(np.ravel_multi_index((z, x // 2, c, y, x % 2), SIZES))))
    return pairs


def from_y(array, d):
    return lax.ppermute(array, AXES, permutation(lambda z, x, c, y: (z, x, c, y - d)))


def to_y(array, d):
    return lax.ppermute(array, AXES, permutation(lambda z, x, c, y: (z, x, c, y + d)))


def swap_xl(array):
    return lax.ppermute(array, AXES, permutation(lambda z, x, c, y: (z, x ^ 1, c, y)))


def swap_core(array):
    return lax.ppermute(array, AXES, permutation(lambda z, x, c, y: (z, x, 1 - c, y)))


def from_first(array, d):
    return lax.ppermute(
        array, AXES, permutation(lambda z, x, c, y: (z - d * c, x - d * (1 - c), c, y))
    )


def from_second(array, d):
    return lax.ppermute(
        array, AXES, permutation(lambda z, x, c, y: (z - d * (1 - c), x - d * c, c, y))
    )


def gather_weight(shard):
    first = jnp.stack([shard] + [from_first(shard, d) for d in range(1, RING)])
    own = [first] + [from_second(first, d) for d in range(1, RING)]
    return own + [swap_core(part) for part in own]


def places(coords):
    z, x, c = coords[0], coords[1], coords[2]
    found = []
    for other in range(2):
        core = c + other - 2 * c * other
        for j in range(RING):
            for i in range(RING):
                dx, dz = i + core * (j - i), j + core * (i - j)
                px, pz = lax.rem(x + dx, RING), lax.rem(z + dz, RING)
                s = pz * 4 + lax.div(px, 2) * 2 + core
                found.append((other * RING + j, i, s, lax.rem(px, 2)))
    return found


def out_copies(coords, refs, weight, sems):
    copies = []
    for n, (array, entry, s, xl) in enumerate(places(coords)):
        rows = pl.ds(pl.multiple_of(xl * 512, 512), 512)
        copies.append(
            pltpu.make_async_copy(refs[array].at[entry], weight.at[s, rows], sems.at[n])
        )
    return copies


def project_out(context, weight, outs):
    def step(s, carry):
        part = jnp.dot(context[...], weight[s], preferred_element_type=jnp.float32)
        part = part.astype(jnp.bfloat16)
        columns = pl.ds(pl.multiple_of(s * 256, 256), 256)
        for d in range(RING):
            outs[d][:, columns] = part[d * 128 : (d + 1) * 128]
        return carry

    lax.fori_loop(0, 16, step, 0)


def spatial_out_kernel(coords, own, other, *rest):
    refs, outs, (context, weight, ctx_sems, sems) = rest[:8], rest[8:12], rest[12:]
    y, xl = coords[3], coords[4]
    copies = out_copies(coords, refs, weight, sems)
    for copy in copies:
        copy.start()
    context_copies = []
    for d in range(RING):
        block = lax.rem(y + d, RING)
        for n, (source, half) in enumerate(((own, xl), (other, 1 - xl))):
            columns = pl.ds(pl.multiple_of(half * 512, 512), 512)
            context_copies.append(
                pltpu.make_async_copy(
                    source.at[block],
                    context.at[pl.ds(d * 128, 128), columns],
                    ctx_sems.at[2 * d + n],
                )
            )
    for copy in context_copies:
        copy.start()
    for copy in context_copies:
        copy.wait()
    for copy in copies:
        copy.wait()
    project_out(context, weight, outs)


def spatial_out_call(coords, own, other, weights):
    anywhere = pl.BlockSpec(memory_space=pl.ANY)
    return pl.pallas_call(
        spatial_out_kernel,
        out_shape=[jax.ShapeDtypeStruct((128, 4096), jnp.bfloat16)] * RING,
        in_specs=[pl.BlockSpec(memory_space=pltpu.SMEM)] + [anywhere] * 10,
        out_specs=[pl.BlockSpec(memory_space=pltpu.VMEM)] * RING,
        scratch_shapes=[
            pltpu.VMEM((512, 1024), jnp.bfloat16),
            pltpu.VMEM((16, 1024, 256), jnp.bfloat16),
            pltpu.SemaphoreType.DMA((8,)),
            pltpu.SemaphoreType.DMA((32,)),
        ],
        compiler_params=pltpu.CompilerParams(vmem_limit_bytes=VMEM_LIMIT),
        cost_estimate=pl.CostEstimate(
            flops=2 * 512 * 1024 * 4096, bytes_accessed=14 << 20, transcendentals=0
        ),
        name="spatial_out",
    )(coords, own, other, *weights)


def temporal_kernel(coords, *rest):
    blocks, qkv_refs, out_refs = rest[:4], rest[4:12], rest[12:20]
    outs = rest[20:24]
    tokens, weight, out_weight, projected, context, token_sems, sems, out_sems = rest[24:]
    token_copies = [
        pltpu.make_async_copy(
            blocks[d], tokens.at[pl.ds(d * 128, 128)], token_sems.at[d]
        )
        for d in range(RING)
    ]
    for copy in token_copies:
        copy.start()
    spots = places(coords)
    copies = [[], [], []]
    for w in range(3):
        for n, (array, entry, s, xl) in enumerate(spots):
            rows = pl.ds(pl.multiple_of(s * 256, 256), 256)
            copies[w].append(
                pltpu.make_async_copy(
                    qkv_refs[array].at[entry, w], weight.at[w, xl, rows], sems.at[w, n]
                )
            )
        for copy in copies[w]:
            copy.start()
    last_copies = out_copies(coords, out_refs, out_weight, out_sems)
    for copy in last_copies:
        copy.start()
    for copy in token_copies:
        copy.wait()
    for w in range(3):
        for copy in copies[w]:
            copy.wait()

        def project(n, carry, w=w):
            xl = lax.div(n, 2)
            columns = pl.ds(pl.multiple_of(lax.rem(n, 2) * 256, 256), 256)
            part = jnp.dot(
                tokens[...], weight[w, xl, :, columns], preferred_element_type=jnp.float32
            )
            projected[w, :, pl.ds(pl.multiple_of(n * 256, 256), 256)] = part.astype(
                jnp.bfloat16
            )
            return carry

        lax.fori_loop(0, 4, project, 0)

    video = lax.rem(lax.div(lax.broadcasted_iota(jnp.int32, (128, 128), 0), 2), 4)
    video_key = lax.rem(lax.div(lax.broadcasted_iota(jnp.int32, (128, 128), 1), 2), 4)
    same = video == video_key

    def attend_block(d, carry):
        rows = pl.ds(pl.multiple_of(d * 128, 128), 128)
        for head in range(8):
            columns = pl.ds(head * HDIM, HDIM)
            query, key, value = (projected[w, rows, columns] for w in range(3))
            scores = lax.dot_general(
                query, key, (((1,), (1,)), ((), ())), preferred_element_type=jnp.float32
            ) * HDIM ** (-0.5)
            exponent = jnp.where(same, jnp.exp(scores), 0.0)
            weights = exponent / jnp.sum(exponent, axis=-1, keepdims=True)
            context[rows, columns] = jnp.dot(
                weights.astype(jnp.bfloat16), value, preferred_element_type=jnp.float32
            ).astype(jnp.bfloat16)
        return carry

    lax.fori_loop(0, RING, attend_block, 0)
    for copy in last_copies:
        copy.wait()
    project_out(context, out_weight, outs)


def temporal_call(coords, blocks, qkv, out_weights):
    anywhere = pl.BlockSpec(memory_space=pl.ANY)
    return pl.pallas_call(
        temporal_kernel,
        out_shape=[jax.ShapeDtypeStruct((128, 4096), jnp.bfloat16)] * RING,
        in_specs=[pl.BlockSpec(memory_space=pltpu.SMEM)] + [anywhere] * 20,
        out_specs=[pl.BlockSpec(memory_space=pltpu.VMEM)] * RING,
        scratch_shapes=[
            pltpu.VMEM((512, 4096), jnp.bfloat16),
            pltpu.VMEM((3, 2, 4096, 512), jnp.bfloat16),
            pltpu.VMEM((16, 1024, 256), jnp.bfloat16),
            pltpu.VMEM((3, 512, 1024), jnp.bfloat16),
            pltpu.VMEM((512, 1024), jnp.bfloat16),
            pltpu.SemaphoreType.DMA((4,)),
            pltpu.SemaphoreType.DMA((3, 32)),
            pltpu.SemaphoreType.DMA((32,)),
        ],
        compiler_params=pltpu.CompilerParams(vmem_limit_bytes=VMEM_LIMIT),
        cost_estimate=pl.CostEstimate(
            flops=2 * 512 * 4096 * 4096, bytes_accessed=40 << 20, transcendentals=512 * 1024
        ),
        name="temporal",
    )(coords, *blocks, *qkv, *out_weights)


def attend(queries, keys_in, values_in):
    head_total = queries.shape[-1] // HDIM
    shaped = [
        member.reshape(member.shape[:2] + (head_total, HDIM))
        for member in (queries, keys_in, values_in)
    ]
    scores = jnp.einsum(
        "ighc,jghc->ghij", shaped[0], shaped[1], preferred_element_type=jnp.float32
    ) * HDIM ** (-0.5)
    exponent = jnp.exp(scores)
    weights = (exponent / jnp.sum(exponent, axis=-1, keepdims=True)).astype(jnp.bfloat16)
    context = jnp.einsum(
        "ghij,jghc->ighc", weights, shaped[2], preferred_element_type=jnp.float32
    )
    return context.astype(jnp.bfloat16).reshape(queries.shape)


def layer_norm(values_in):
    values_f = values_in.astype(jnp.float32)
    centred = values_f - jnp.mean(values_f, axis=-1, keepdims=True)
    variance = jnp.mean(centred * centred, axis=-1, keepdims=True)
    return (centred * lax.rsqrt(variance + 1e-06)).astype(jnp.bfloat16)


def sum_over_y(parts):
    total = parts[0].astype(jnp.float32)
    for d in range(1, RING):
        total = total + to_y(parts[d], d).astype(jnp.float32)
    return total


def shards(
    residual,
    spatial_query,
    spatial_key,
    spatial_value,
    spatial_out,
    temporal_query,
    temporal_key,
    temporal_value,
    temporal_out,
):
    z, xh, c, y, xl = (lax.axis_index(name) for name in AXES)
    coords = jnp.stack([z, 2 * xh + xl, c, y, xl]).astype(jnp.int32)
    spatial_weights = gather_weight(spatial_out)
    qkv_weights = gather_weight(jnp.stack([temporal_query, temporal_key, temporal_value]))
    out_weights = gather_weight(temporal_out)

    layout = (128, 8, 512)
    context = attend(
        spatial_query.reshape(layout), spatial_key.reshape(layout), spatial_value.reshape(layout)
    ).reshape(RING, 2, 128, 512)
    own = lax.dynamic_index_in_dim(context, xl, axis=1, keepdims=False)
    other = swap_xl(lax.dynamic_index_in_dim(context, 1 - xl, axis=1, keepdims=False))
    parts = spatial_out_call(coords, own, other, spatial_weights)
    middle = (residual.reshape(128, 4096).astype(jnp.float32) + sum_over_y(parts)).astype(
        jnp.bfloat16
    )
    normed = layer_norm(middle).reshape(16, 8, 4096)
    normed = lax.all_to_all(
        normed, ("z", "xh", "c"), split_axis=0, concat_axis=0, tiled=True
    ).reshape(128, 4096)
    blocks = [normed] + [from_y(normed, d) for d in range(1, RING)]
    parts = temporal_call(coords, blocks, qkv_weights, out_weights)
    summed = sum_over_y(parts).astype(jnp.bfloat16).reshape(16, 8, 4096)
    summed = lax.all_to_all(summed, ("z", "xh", "c"), split_axis=0, concat_axis=0, tiled=True)
    finished = middle.astype(jnp.float32) + summed.reshape(128, 4096).astype(jnp.float32)
    return finished.astype(jnp.bfloat16).reshape(residual.shape)


def solution(mesh):
    split = Mesh(mesh.devices.reshape(SIZES), AXES)
    seq, head = ("z", "xh", "c"), ("y", "xl")
    in_specs = (
        P(head, None, seq, None),
        P(None, None, seq, head),
        P(None, None, seq, head),
        P(None, None, seq, head),
        P(head, seq),
        P(seq, head),
        P(seq, head),
        P(seq, head),
        P(head, seq),
    )
    out_specs = P(head, None, seq, None)
    return jax.shard_map(shards, mesh=split, in_specs=in_specs, out_specs=out_specs, check_vma=False)
```

```python
import numpy as np

import jax
import jax.numpy as jnp
from jax import lax
from jax.experimental import pallas as pl
from jax.experimental.pallas import tpu as pltpu
from jax.sharding import Mesh
from jax.sharding import PartitionSpec as P

HDIM = 128
AXES = ("z", "xh", "c", "y", "xl")
SIZES = (4, 2, 2, 4, 2)
RING = 4
SHORT = pl.CostEstimate(flops=1 << 20, bytes_accessed=1 << 16, transcendentals=0)
VMEM_LIMIT = 28 * 1024 * 1024


def permutation(move):
    pairs = []
    for source in range(int(np.prod(SIZES))):
        z, xh, c, y, xl = (int(v) for v in np.unravel_index(source, SIZES))
        z, x, c, y = (v % n for v, n in zip(move(z, 2 * xh + xl, c, y), (4, 4, 2, 4)))
        pairs.append((source, int(np.ravel_multi_index((z, x // 2, c, y, x % 2), SIZES))))
    return pairs


def from_y(array, d):
    return lax.ppermute(array, AXES, permutation(lambda z, x, c, y: (z, x, c, y - d)))


def to_y(array, d):
    return lax.ppermute(array, AXES, permutation(lambda z, x, c, y: (z, x, c, y + d)))


def swap_xl(array):
    return lax.ppermute(array, AXES, permutation(lambda z, x, c, y: (z, x ^ 1, c, y)))


def swap_core(array):
    return lax.ppermute(array, AXES, permutation(lambda z, x, c, y: (z, x, 1 - c, y)))


def from_first(array, d):
    return lax.ppermute(
        array, AXES, permutation(lambda z, x, c, y: (z - d * c, x - d * (1 - c), c, y))
    )


def from_second(array, d):
    return lax.ppermute(
        array, AXES, permutation(lambda z, x, c, y: (z - d * (1 - c), x - d * c, c, y))
    )


def after(array, *others):
    return lax.optimization_barrier((array,) + others)[0]


def ring_spots(coords, spots):
    z, x, c = coords[0], coords[1], coords[2]
    found = []
    for n, (j, first, count) in enumerate(spots):
        for k in range(count):
            i = first + k
            px = lax.rem(x + i + c * (j - i), RING)
            pz = lax.rem(z + j + c * (i - j), RING)
            found.append((n, k, pz * 2 + lax.div(px, 2), lax.rem(px, 2)))
    return found


def load(coords, pieces, shapes, copies_of, name, previous=()):
    count = len(shapes)

    def kernel(coords, *rest):
        refs, weights, sems = rest[: len(pieces)], rest[-1 - count : -1], rest[-1]
        copies = [
            pltpu.make_async_copy(source, target, sems.at[n])
            for n, (source, target) in enumerate(copies_of(coords, refs, weights))
        ]
        for copy in copies:
            copy.start()
        for copy in copies:
            copy.wait()

    in_vmem = pl.BlockSpec(memory_space=pltpu.VMEM)
    return pl.pallas_call(
        kernel,
        out_shape=[pltpu.VMEM(shape, jnp.bfloat16) for shape in shapes],
        in_specs=[pl.BlockSpec(memory_space=pltpu.SMEM)]
        + [pl.BlockSpec(memory_space=pltpu.HBM)] * len(pieces)
        + [in_vmem] * len(previous),
        out_specs=[in_vmem] * count,
        input_output_aliases={1 + len(pieces) + n: n for n in range(len(previous))},
        scratch_shapes=[pltpu.SemaphoreType.DMA((32 * count,))],
        compiler_params=pltpu.CompilerParams(vmem_limit_bytes=VMEM_LIMIT),
        cost_estimate=SHORT,
        name=name,
    )(
        coords,
        *[pltpu.with_memory_space_constraint(piece, pltpu.HBM) for piece in pieces],
        *[pltpu.with_memory_space_constraint(array, pltpu.VMEM) for array in previous],
    )


def load_temporal(coords, pieces, spots, previous=()):
    def copies(coords, refs, weights):
        for n, entry, zx, xl in ring_spots(coords, spots):
            for r in range(2):
                s = zx * 2 + coords[2] + r - 2 * r * coords[2]
                rows = pl.ds(pl.multiple_of(s * 256, 256), 256)
                for w, weight in enumerate(weights[:3]):
                    yield refs[n].at[entry, 4 * r + w], weight.at[xl, rows]
                yield refs[n].at[entry, 4 * r + 3], weights[3].at[s, xl]

    shapes = [(2, 4096, 256)] * 3 + [(16, 2, 256, 256)]
    return load(coords, pieces, shapes, copies, "load_temporal", previous)


def load_out(coords, pieces):
    def copies(coords, refs, weights):
        for n, entry, zx, xl in ring_spots(coords, [(j, 0, RING) for j in range(RING)]):
            yield refs[n].at[entry], weights[0].at[zx, pl.ds(xl * 2, 2)]

    return load(coords, pieces, [(8, 4, 256, 256)], copies, "load_out")[0]


def project_out(context, weight, outs):
    starts = np.cumsum([0] + [out.shape[0] for out in outs])

    def step(n, carry):
        part = jnp.dot(
            context[...], weight[n].reshape(-1, 256), preferred_element_type=jnp.float32
        ).astype(jnp.bfloat16)
        columns = pl.ds(pl.multiple_of(n * 256, 256), 256)
        for start, out in zip(starts, outs):
            out[:, columns] = part[start : start + out.shape[0]]
        return carry

    lax.fori_loop(0, weight.shape[0], step, 0)


def spatial_out_kernel(coords, *rest):
    sources, weight, outs, context = rest[:4], rest[4], rest[5:-1], rest[-1]
    y, xl = coords[3], coords[4]
    for d in range(RING):
        block = lax.rem(y + d, RING)
        for n, source in enumerate(sources):
            half = xl + (n % 2) * (1 - 2 * xl)
            columns = pl.ds(pl.multiple_of(half * 512, 512), 512)
            start = d * 256 + (n // 2) * 128
            context[start : start + 128, columns] = source[block]
    project_out(context, weight, outs)


def spatial_out_call(coords, sources, weight):
    in_vmem = pl.BlockSpec(memory_space=pltpu.VMEM)
    return pl.pallas_call(
        spatial_out_kernel,
        out_shape=[jax.ShapeDtypeStruct((256, 2048), jnp.bfloat16)] * RING,
        in_specs=[pl.BlockSpec(memory_space=pltpu.SMEM)] + [in_vmem] * 5,
        out_specs=[in_vmem] * RING,
        scratch_shapes=[pltpu.VMEM((1024, 1024), jnp.bfloat16)],
        compiler_params=pltpu.CompilerParams(vmem_limit_bytes=VMEM_LIMIT),
        cost_estimate=SHORT,
        name="spatial_out",
    )(coords, *sources, pltpu.with_memory_space_constraint(weight, pltpu.VMEM))


def temporal_call(blocks, weights):
    sizes = [block.shape[0] for block in blocks]
    total = sum(sizes)
    count = total // 128
    shapes = [(128, 4096)] * (count // 2) + [(64 * count, 4096)]

    def kernel(*rest):
        tokens, rest = rest[: len(sizes)], rest[len(sizes) :]
        weights, last, outs = rest[:3], rest[3], rest[4:-3]
        rows, projected, context = rest[-3:]
        start = 0
        for token, size in zip(tokens, sizes):
            rows[start : start + size] = token[...]
            start += size

        for w, weight in enumerate(weights):

            def project(n, carry, w=w, weight=weight):
                part = jnp.dot(rows[...], weight[n], preferred_element_type=jnp.float32)
                columns = pl.ds(pl.multiple_of(n * 256, 256), 256)
                projected[w, :, columns] = part.astype(jnp.bfloat16)
                return carry

            lax.fori_loop(0, 2, project, 0)
        video = lax.rem(lax.div(lax.broadcasted_iota(jnp.int32, (128, 128), 0), 2), 4)
        video_key = lax.rem(lax.div(lax.broadcasted_iota(jnp.int32, (128, 128), 1), 2), 4)
        same = video == video_key
        heads = [slice(h * HDIM, (h + 1) * HDIM) for h in range(4)]
        for b in range(count):
            at = slice(b * 128, (b + 1) * 128)
            scores = [
                lax.dot_general(
                    projected[0, at, h],
                    projected[1, at, h],
                    (((1,), (1,)), ((), ())),
                    preferred_element_type=jnp.float32,
                )
                for h in heads
            ]
            exponents = [jnp.where(same, jnp.exp(s * HDIM ** (-0.5)), 0.0) for s in scores]
            shares = [
                (e / jnp.sum(e, axis=-1, keepdims=True)).astype(jnp.bfloat16) for e in exponents
            ]
            for h, share in zip(heads, shares):
                context[at, h] = jnp.dot(
                    share, projected[2, at, h], preferred_element_type=jnp.float32
                ).astype(jnp.bfloat16)
        project_out(context, last, outs)

    in_vmem = pl.BlockSpec(memory_space=pltpu.VMEM)
    return pl.pallas_call(
        kernel,
        out_shape=[jax.ShapeDtypeStruct(shape, jnp.bfloat16) for shape in shapes],
        in_specs=[in_vmem] * (len(sizes) + 4),
        out_specs=[in_vmem] * len(shapes),
        scratch_shapes=[
            pltpu.VMEM((total, 4096), jnp.bfloat16),
            pltpu.VMEM((3, total, 512), jnp.bfloat16),
            pltpu.VMEM((total, 512), jnp.bfloat16),
        ],
        compiler_params=pltpu.CompilerParams(vmem_limit_bytes=VMEM_LIMIT),
        cost_estimate=SHORT,
        name="temporal",
    )(
        *blocks,
        *[pltpu.with_memory_space_constraint(w, pltpu.VMEM) for w in weights],
    )


def spatial_scores(queries, keys_in, values_in):
    shaped = [
        member.reshape(member.shape[:2] + (-1, HDIM)) for member in (queries, keys_in, values_in)
    ]
    scores = jnp.einsum(
        "ighc,jghc->ghij", shaped[0], shaped[1], preferred_element_type=jnp.float32
    ) * HDIM ** (-0.5)
    exponent = jnp.exp(scores)
    weights = (exponent / jnp.sum(exponent, axis=-1, keepdims=True)).astype(jnp.bfloat16)
    return weights, shaped[2]


def spatial_context(weights, values_in):
    context = jnp.einsum(
        "ghij,jghc->ighc", weights, values_in, preferred_element_type=jnp.float32
    )
    return context.astype(jnp.bfloat16)


def norm_call(coords, residual, mine, other):
    def kernel(coords, res, mine, other, middle, normed, total):
        c = coords[2]
        for n in range(8):
            for part, core in ((mine, c), (other, 1 - c)):
                columns = pl.ds(pl.multiple_of(n * 512 + core * 256, 256), 256)
                total[:, columns] = part[:, n * 256 : (n + 1) * 256]

        def step(n, carry):
            rows = pl.ds(pl.multiple_of(n * 16, 16), 16)
            summed = res[rows].astype(jnp.float32) + total[rows].astype(jnp.float32)
            rounded = summed.astype(jnp.bfloat16)
            middle[rows] = rounded
            values = rounded.astype(jnp.float32)
            centred = values - jnp.mean(values, axis=-1, keepdims=True)
            variance = jnp.mean(centred * centred, axis=-1, keepdims=True)
            normed[rows] = (centred * lax.rsqrt(variance + 1e-06)).astype(jnp.bfloat16)
            return carry

        lax.fori_loop(0, 8, step, 0)

    in_vmem = pl.BlockSpec(memory_space=pltpu.VMEM)
    rows = jax.ShapeDtypeStruct((128, 4096), jnp.bfloat16)
    return pl.pallas_call(
        kernel,
        out_shape=[rows, rows],
        in_specs=[pl.BlockSpec(memory_space=pltpu.SMEM)] + [in_vmem] * 3,
        out_specs=[in_vmem] * 2,
        scratch_shapes=[pltpu.VMEM((128, 4096), jnp.bfloat16)],
        compiler_params=pltpu.CompilerParams(vmem_limit_bytes=VMEM_LIMIT),
        cost_estimate=SHORT,
        name="norm",
    )(coords, residual, mine, other)


def shards(
    residual,
    spatial_query,
    spatial_key,
    spatial_value,
    spatial_out,
    temporal_query,
    temporal_key,
    temporal_value,
    temporal_out,
):
    z, xh, c, y, xl = (lax.axis_index(name) for name in AXES)
    coords = jnp.stack([z, 2 * xh + xl, c, y, xl]).astype(jnp.int32)

    layout = (128, 8, 512)
    scores, values_in = spatial_scores(
        *(array.reshape(layout) for array in (spatial_query, spatial_key, spatial_value))
    )

    context = spatial_context(scores, values_in).reshape(RING, 2, 128, 512)
    own, other = (
        lax.dynamic_index_in_dim(context, which, axis=1, keepdims=False) for which in (xl, 1 - xl)
    )

    out_shard = spatial_out.reshape(2, 256, 256)
    out_first = jnp.stack([out_shard] + [from_first(out_shard, d) for d in range(1, RING)])
    out_first, own, other = lax.optimization_barrier((out_first, own, other))
    out_own = [out_first] + [from_second(out_first, d) for d in range(1, RING)]
    other = swap_xl(other)
    sources = [own, other, swap_core(own)]
    *sources, o_1, o_2, o_3 = lax.optimization_barrier((*sources, *out_own[1:]))
    out_own[1:] = o_1, o_2, o_3
    sources.append(swap_core(sources[1]))
    tiles = jnp.stack(
        [w.reshape(256, 2, 256) for w in (temporal_query, temporal_key, temporal_value)]
        + [temporal_out.reshape(2, 256, 256).swapaxes(0, 1)]
    ).transpose(2, 0, 1, 3)
    mine, theirs = (
        lax.dynamic_index_in_dim(tiles, which, axis=0, keepdims=False) for which in (c, 1 - c)
    )
    shard = after(jnp.concatenate([mine, swap_core(theirs)]), *out_own[1:])
    shards_first = [shard] + [from_first(shard, d) for d in range(1, RING)]
    *sources, residual_rows = lax.optimization_barrier((*sources, residual.reshape(128, 4096)))
    parts = spatial_out_call(coords, sources, load_out(coords, out_own))

    far = [to_y(parts[2][:128], 1), to_y(parts[2][128:], -1)]
    near_p = jnp.concatenate([parts[1][:128] + far[0], parts[1][128:]])
    near_m = jnp.concatenate([parts[3][:128], parts[3][128:] + far[1]])
    first = jnp.stack(lax.optimization_barrier((*shards_first, *far))[:RING])
    first, near_p, near_m = lax.optimization_barrier((first, near_p, near_m))
    pieces = [first, from_second(first, 1), from_second(first, -1)]
    total = parts[0].astype(jnp.float32)
    for part in (to_y(near_p, 1), to_y(near_m, -1)):
        total = total + part.astype(jnp.float32)
    total = total.astype(jnp.bfloat16)
    middle, normed = norm_call(coords, residual_rows, total[:128], swap_core(total[128:]))
    normed = lax.all_to_all(
        normed.reshape(16, 8, 4096), ("z", "xh", "c"), split_axis=0, concat_axis=0, tiled=True
    ).reshape(128, 4096)
    normed, *pieces = lax.optimization_barrier((normed, *pieces))
    next_p, next_m = from_y(normed, 1), from_y(normed, -1)
    last = [from_second(pieces[1][:2], 1), from_second(pieces[2][2:], -1)]
    weights = load_temporal(coords, pieces, [(j, 0, RING) for j in (0, 1, 3)])
    *last, next_p, next_m, w_0, w_1, w_2, w_3 = lax.optimization_barrier(
        (*last, next_p, next_m, *weights)
    )
    weights = [w_0, w_1, w_2, w_3]
    weights = load_temporal(coords, last, [(2, 0, 2), (2, 2, 2)], weights)

    far = [from_y(next_p[:64], 1), from_y(next_m[64:], -1)]
    *far, w_0, w_1, w_2, w_3 = lax.optimization_barrier((*far, *weights))
    weights = [w_0, w_1, w_2, w_3]

    def both_cores(blocks):
        *parts, others = temporal_call(blocks + [swap_core(block) for block in blocks], weights)
        others = swap_core(others)
        return [
            part.astype(jnp.float32) + others[128 * n : 128 * (n + 1)].astype(jnp.float32)
            for n, part in enumerate(parts)
        ]

    part_p, part_m, part_far = both_cores([next_p, next_m] + far)
    part_far = part_far.astype(jnp.bfloat16)
    far = [to_y(part_far[:64], 1), to_y(part_far[64:], -1)]
    zeros = jnp.zeros((64, 4096), jnp.bfloat16)
    part_p += jnp.concatenate([far[0], zeros]).astype(jnp.float32)
    part_m += jnp.concatenate([zeros, far[1]]).astype(jnp.float32)
    (total,) = both_cores([normed])
    for part, d in ((part_p, 1), (part_m, -1)):
        total = total + to_y(part.astype(jnp.bfloat16), d).astype(jnp.float32)
    summed = total.astype(jnp.bfloat16).reshape(16, 8, 4096)
    summed = lax.all_to_all(summed, ("z", "xh", "c"), split_axis=0, concat_axis=0, tiled=True)
    finished = middle.astype(jnp.float32) + summed.reshape(128, 4096).astype(jnp.float32)
    return finished.astype(jnp.bfloat16).reshape(residual.shape)


def solution(mesh):
    split = Mesh(mesh.devices.reshape(SIZES), AXES)
    seq, head = ("z", "xh", "c"), ("y", "xl")
    in_specs = (
        P(head, None, seq, None),
        P(None, None, seq, head),
        P(None, None, seq, head),
        P(None, None, seq, head),
        P(head, seq),
        P(seq, head),
        P(seq, head),
        P(seq, head),
        P(head, seq),
    )
    out_specs = P(head, None, seq, None)
    return jax.shard_map(shards, mesh=split, in_specs=in_specs, out_specs=out_specs, check_vma=False)
```

```python
import numpy as np

import jax
import jax.numpy as jnp
from jax import lax
from jax.experimental import pallas as pl
from jax.experimental.pallas import tpu as pltpu
from jax.sharding import Mesh
from jax.sharding import PartitionSpec as P

HDIM = 128
AXES = ("z", "xh", "c", "y", "xl")
SIZES = (4, 2, 2, 4, 2)
RING = 4
SHORT = pl.CostEstimate(flops=1 << 20, bytes_accessed=1 << 16, transcendentals=0)
VMEM_LIMIT = 28 * 1024 * 1024


def permutation(move):
    pairs = []
    for source in range(int(np.prod(SIZES))):
        z, xh, c, y, xl = (int(v) for v in np.unravel_index(source, SIZES))
        z, x, c, y = (v % n for v, n in zip(move(z, 2 * xh + xl, c, y), (4, 4, 2, 4)))
        pairs.append((source, int(np.ravel_multi_index((z, x // 2, c, y, x % 2), SIZES))))
    return pairs


def from_y(array, d):
    return lax.ppermute(array, AXES, permutation(lambda z, x, c, y: (z, x, c, y - d)))


def to_y(array, d):
    return lax.ppermute(array, AXES, permutation(lambda z, x, c, y: (z, x, c, y + d)))


def swap_xl(array):
    return lax.ppermute(array, AXES, permutation(lambda z, x, c, y: (z, x ^ 1, c, y)))


def swap_core(array):
    return lax.ppermute(array, AXES, permutation(lambda z, x, c, y: (z, x, 1 - c, y)))


def from_first(array, d):
    return lax.ppermute(
        array, AXES, permutation(lambda z, x, c, y: (z - d * c, x - d * (1 - c), c, y))
    )


def from_second(array, d):
    return lax.ppermute(
        array, AXES, permutation(lambda z, x, c, y: (z - d * (1 - c), x - d * c, c, y))
    )


def after(array, *others):
    return lax.optimization_barrier((array,) + others)[0]


def ring_spots(coords, spots):
    z, x, c = coords[0], coords[1], coords[2]
    found = []
    for n, (j, first, count) in enumerate(spots):
        for k in range(count):
            i = first + k
            px = lax.rem(x + i + c * (j - i), RING)
            pz = lax.rem(z + j + c * (i - j), RING)
            found.append((n, k, pz * 2 + lax.div(px, 2), lax.rem(px, 2)))
    return found


def load(coords, pieces, shapes, copies_of, name, previous=()):
    count = len(shapes)

    def kernel(coords, *rest):
        refs, weights, sems = rest[: len(pieces)], rest[-1 - count : -1], rest[-1]
        copies = [
            pltpu.make_async_copy(source, target, sems.at[n])
            for n, (source, target) in enumerate(copies_of(coords, refs, weights))
        ]
        for copy in copies:
            copy.start()
        for copy in copies:
            copy.wait()

    in_vmem = pl.BlockSpec(memory_space=pltpu.VMEM)
    return pl.pallas_call(
        kernel,
        out_shape=[pltpu.VMEM(shape, jnp.bfloat16) for shape in shapes],
        in_specs=[pl.BlockSpec(memory_space=pltpu.SMEM)]
        + [pl.BlockSpec(memory_space=pltpu.HBM)] * len(pieces)
        + [in_vmem] * len(previous),
        out_specs=[in_vmem] * count,
        input_output_aliases={1 + len(pieces) + n: n for n in range(len(previous))},
        scratch_shapes=[pltpu.SemaphoreType.DMA((32 * count,))],
        compiler_params=pltpu.CompilerParams(vmem_limit_bytes=VMEM_LIMIT),
        cost_estimate=SHORT,
        name=name,
    )(
        coords,
        *[pltpu.with_memory_space_constraint(piece, pltpu.HBM) for piece in pieces],
        *[pltpu.with_memory_space_constraint(array, pltpu.VMEM) for array in previous],
    )


def load_temporal(coords, pieces, spots, previous=()):
    def copies(coords, refs, weights):
        for n, entry, zx, xl in ring_spots(coords, spots):
            for r in range(2):
                s = zx * 2 + coords[2] + r - 2 * r * coords[2]
                rows = pl.ds(pl.multiple_of(s * 256, 256), 256)
                for w, weight in enumerate(weights[:3]):
                    yield refs[n].at[entry, 4 * r + w], weight.at[xl, rows]
                yield refs[n].at[entry, 4 * r + 3], weights[3].at[s, xl]

    shapes = [(2, 4096, 256)] * 3 + [(16, 2, 256, 256)]
    return load(coords, pieces, shapes, copies, "load_temporal", previous)


def load_out(coords, pieces):
    def copies(coords, refs, weights):
        for n, entry, zx, xl in ring_spots(coords, [(j, 0, RING) for j in range(RING)]):
            yield refs[n].at[entry], weights[0].at[zx, pl.ds(xl * 2, 2)]

    return load(coords, pieces, [(8, 4, 256, 256)], copies, "load_out")[0]


def project_out(context, weight, outs):
    starts = np.cumsum([0] + [out.shape[0] for out in outs])

    def step(n, carry):
        part = jnp.dot(
            context[...], weight[n].reshape(-1, 256), preferred_element_type=jnp.float32
        ).astype(jnp.bfloat16)
        columns = pl.ds(pl.multiple_of(n * 256, 256), 256)
        for start, out in zip(starts, outs):
            out[:, columns] = part[start : start + out.shape[0]]
        return carry

    lax.fori_loop(0, weight.shape[0], step, 0)


def spatial_out_kernel(coords, *rest):
    sources, weight, outs, context = rest[:4], rest[4], rest[5:-1], rest[-1]
    y, xl = coords[3], coords[4]
    for d in range(RING):
        block = lax.rem(y + d, RING)
        for n, source in enumerate(sources):
            half = xl + (n % 2) * (1 - 2 * xl)
            columns = pl.ds(pl.multiple_of(half * 512, 512), 512)
            start = d * 256 + (n // 2) * 128
            context[start : start + 128, columns] = source[block]
    project_out(context, weight, outs)


def spatial_out_call(coords, sources, weight):
    in_vmem = pl.BlockSpec(memory_space=pltpu.VMEM)
    return pl.pallas_call(
        spatial_out_kernel,
        out_shape=[jax.ShapeDtypeStruct((256, 2048), jnp.bfloat16)] * RING,
        in_specs=[pl.BlockSpec(memory_space=pltpu.SMEM)] + [in_vmem] * 5,
        out_specs=[in_vmem] * RING,
        scratch_shapes=[pltpu.VMEM((1024, 1024), jnp.bfloat16)],
        compiler_params=pltpu.CompilerParams(vmem_limit_bytes=VMEM_LIMIT),
        cost_estimate=SHORT,
        name="spatial_out",
    )(coords, *sources, pltpu.with_memory_space_constraint(weight, pltpu.VMEM))


def temporal_call(blocks, weights):
    sizes = [block.shape[0] for block in blocks]
    total = sum(sizes)
    count = total // 128
    shapes = [(128, 4096)] * (count // 2) + [(64 * count, 4096)]

    def kernel(*rest):
        tokens, rest = rest[: len(sizes)], rest[len(sizes) :]
        weights, last, outs = rest[:3], rest[3], rest[4:-3]
        rows, projected, context = rest[-3:]
        start = 0
        for token, size in zip(tokens, sizes):
            rows[start : start + size] = token[...]
            start += size

        for w, weight in enumerate(weights):

            def project(n, carry, w=w, weight=weight):
                part = jnp.dot(rows[...], weight[n], preferred_element_type=jnp.float32)
                columns = pl.ds(pl.multiple_of(n * 256, 256), 256)
                projected[w, :, columns] = part.astype(jnp.bfloat16)
                return carry

            lax.fori_loop(0, 2, project, 0)
        video = lax.rem(lax.div(lax.broadcasted_iota(jnp.int32, (128, 128), 0), 2), 4)
        video_key = lax.rem(lax.div(lax.broadcasted_iota(jnp.int32, (128, 128), 1), 2), 4)
        same = video == video_key
        heads = [slice(h * HDIM, (h + 1) * HDIM) for h in range(4)]
        for b in range(count):
            at = slice(b * 128, (b + 1) * 128)
            scores = [
                lax.dot_general(
                    projected[0, at, h],
                    projected[1, at, h],
                    (((1,), (1,)), ((), ())),
                    preferred_element_type=jnp.float32,
                )
                for h in heads
            ]
            exponents = [jnp.where(same, jnp.exp(s * HDIM ** (-0.5)), 0.0) for s in scores]
            shares = [
                (e / jnp.sum(e, axis=-1, keepdims=True)).astype(jnp.bfloat16) for e in exponents
            ]
            for h, share in zip(heads, shares):
                context[at, h] = jnp.dot(
                    share, projected[2, at, h], preferred_element_type=jnp.float32
                ).astype(jnp.bfloat16)
        project_out(context, last, outs)

    in_vmem = pl.BlockSpec(memory_space=pltpu.VMEM)
    return pl.pallas_call(
        kernel,
        out_shape=[jax.ShapeDtypeStruct(shape, jnp.bfloat16) for shape in shapes],
        in_specs=[in_vmem] * (len(sizes) + 4),
        out_specs=[in_vmem] * len(shapes),
        scratch_shapes=[
            pltpu.VMEM((total, 4096), jnp.bfloat16),
            pltpu.VMEM((3, total, 512), jnp.bfloat16),
            pltpu.VMEM((total, 512), jnp.bfloat16),
        ],
        compiler_params=pltpu.CompilerParams(vmem_limit_bytes=VMEM_LIMIT),
        cost_estimate=SHORT,
        name="temporal",
    )(
        *blocks,
        *[pltpu.with_memory_space_constraint(w, pltpu.VMEM) for w in weights],
    )


def spatial_scores(queries, keys_in, values_in):
    shaped = [
        member.reshape(member.shape[:2] + (-1, HDIM)) for member in (queries, keys_in, values_in)
    ]
    scores = jnp.einsum(
        "ighc,jghc->ghij", shaped[0], shaped[1], preferred_element_type=jnp.float32
    ) * HDIM ** (-0.5)
    exponent = jnp.exp(scores)
    weights = (exponent / jnp.sum(exponent, axis=-1, keepdims=True)).astype(jnp.bfloat16)
    return weights, shaped[2]


def spatial_context(weights, values_in):
    context = jnp.einsum(
        "ghij,jghc->ighc", weights, values_in, preferred_element_type=jnp.float32
    )
    return context.astype(jnp.bfloat16)


def norm_call(coords, residual, mine, other):
    def kernel(coords, res, mine, other, middle, normed, total):
        c = coords[2]
        for n in range(8):
            for part, core in ((mine, c), (other, 1 - c)):
                columns = pl.ds(pl.multiple_of(n * 512 + core * 256, 256), 256)
                total[:, columns] = part[:, n * 256 : (n + 1) * 256]

        def step(n, carry):
            rows = pl.ds(pl.multiple_of(n * 16, 16), 16)
            summed = res[rows].astype(jnp.float32) + total[rows].astype(jnp.float32)
            rounded = summed.astype(jnp.bfloat16)
            middle[rows] = rounded
            values = rounded.astype(jnp.float32)
            centred = values - jnp.mean(values, axis=-1, keepdims=True)
            variance = jnp.mean(centred * centred, axis=-1, keepdims=True)
            normed[rows] = (centred * lax.rsqrt(variance + 1e-06)).astype(jnp.bfloat16)
            return carry

        lax.fori_loop(0, 8, step, 0)

    in_vmem = pl.BlockSpec(memory_space=pltpu.VMEM)
    rows = jax.ShapeDtypeStruct((128, 4096), jnp.bfloat16)
    return pl.pallas_call(
        kernel,
        out_shape=[rows, rows],
        in_specs=[pl.BlockSpec(memory_space=pltpu.SMEM)] + [in_vmem] * 3,
        out_specs=[in_vmem] * 2,
        scratch_shapes=[pltpu.VMEM((128, 4096), jnp.bfloat16)],
        compiler_params=pltpu.CompilerParams(vmem_limit_bytes=VMEM_LIMIT),
        cost_estimate=SHORT,
        name="norm",
    )(coords, residual, mine, other)


def shards(
    residual,
    spatial_query,
    spatial_key,
    spatial_value,
    spatial_out,
    temporal_query,
    temporal_key,
    temporal_value,
    temporal_out,
):
    z, xh, c, y, xl = (lax.axis_index(name) for name in AXES)
    coords = jnp.stack([z, 2 * xh + xl, c, y, xl]).astype(jnp.int32)

    layout = (128, 8, 512)
    scores, values_in = spatial_scores(
        *(array.reshape(layout) for array in (spatial_query, spatial_key, spatial_value))
    )

    context = spatial_context(scores, values_in).reshape(RING, 2, 128, 512)
    own, other = (
        lax.dynamic_index_in_dim(context, which, axis=1, keepdims=False) for which in (xl, 1 - xl)
    )

    out_shard = spatial_out.reshape(2, 256, 256)
    out_first = jnp.stack([out_shard] + [from_first(out_shard, d) for d in range(1, RING)])
    out_first, own, other = lax.optimization_barrier((out_first, own, other))
    out_own = [out_first] + [from_second(out_first, d) for d in range(1, RING)]
    other = swap_xl(other)
    sources = [own, other, swap_core(own)]
    *sources, o_1, o_2, o_3, residual_rows = lax.optimization_barrier(
        (*sources, *out_own[1:], residual.reshape(128, 4096))
    )
    out_own[1:] = o_1, o_2, o_3
    sources.append(swap_core(sources[1]))
    tiles = jnp.stack(
        [w.reshape(256, 2, 256) for w in (temporal_query, temporal_key, temporal_value)]
        + [temporal_out.reshape(2, 256, 256).swapaxes(0, 1)]
    ).transpose(2, 0, 1, 3)
    mine, theirs = (
        lax.dynamic_index_in_dim(tiles, which, axis=0, keepdims=False) for which in (c, 1 - c)
    )
    shard = after(jnp.concatenate([mine, swap_core(theirs)]), *out_own[1:])
    shards_first = [shard] + [from_first(shard, d) for d in range(1, RING)]
    parts = spatial_out_call(coords, sources, load_out(coords, out_own))

    far = [to_y(parts[2][:128], 1), to_y(parts[2][128:], -1)]
    near_p = jnp.concatenate([parts[1][:128] + far[0], parts[1][128:]])
    near_m = jnp.concatenate([parts[3][:128], parts[3][128:] + far[1]])
    first = jnp.stack(lax.optimization_barrier((*shards_first, *far))[:RING])
    first, near_p, near_m = lax.optimization_barrier((first, near_p, near_m))
    pieces = [first, from_second(first, 1), from_second(first, -1)]
    total = parts[0].astype(jnp.float32)
    for part in (to_y(near_p, 1), to_y(near_m, -1)):
        total = total + part.astype(jnp.float32)
    total = total.astype(jnp.bfloat16)
    middle, normed = norm_call(coords, residual_rows, total[:128], swap_core(total[128:]))
    normed = lax.all_to_all(
        normed.reshape(16, 8, 4096), ("z", "xh", "c"), split_axis=0, concat_axis=0, tiled=True
    ).reshape(128, 4096)
    normed, *pieces = lax.optimization_barrier((normed, *pieces))
    next_p, next_m = from_y(normed, 1), from_y(normed, -1)
    last = [from_second(pieces[1][:2], 1), from_second(pieces[2][2:], -1)]
    weights = load_temporal(coords, pieces, [(j, 0, RING) for j in (0, 1, 3)])
    *last, next_p, next_m, w_0, w_1, w_2, w_3 = lax.optimization_barrier(
        (*last, next_p, next_m, *weights)
    )
    weights = [w_0, w_1, w_2, w_3]
    weights = load_temporal(coords, last, [(2, 0, 2), (2, 2, 2)], weights)

    far = [from_y(next_p[:64], 1), from_y(next_m[64:], -1)]
    near = [next_p, next_m, swap_core(next_p), swap_core(next_m)]
    *near, own_swapped = lax.optimization_barrier((*near, swap_core(normed)))

    part_p, part_m, others = temporal_call(near, weights)
    *far, part_p, part_m, others = lax.optimization_barrier((*far, part_p, part_m, others))
    others = swap_core(others)
    part, far_others = temporal_call(far + [swap_core(half) for half in far], weights)
    far_others, others = lax.optimization_barrier((far_others, others))
    part = (part.astype(jnp.float32) + swap_core(far_others).astype(jnp.float32)).astype(jnp.bfloat16)
    far = [to_y(part[:64], 1), to_y(part[64:], -1)]
    own, own_others = temporal_call([normed, own_swapped], weights)
    *far, own, own_others = lax.optimization_barrier((*far, own, own_others))
    total = own.astype(jnp.float32) + swap_core(own_others).astype(jnp.float32)
    zeros = jnp.zeros((64, 4096), jnp.bfloat16)
    for d, part, other, passed in (
        (1, part_p, others[:128], [far[0], zeros]),
        (-1, part_m, others[128:], [zeros, far[1]]),
    ):
        part = part.astype(jnp.float32) + other.astype(jnp.float32)
        part = (part + jnp.concatenate(passed).astype(jnp.float32)).astype(jnp.bfloat16)
        total = total + to_y(part, d).astype(jnp.float32)
    summed = total.astype(jnp.bfloat16).reshape(16, 8, 4096)
    summed = lax.all_to_all(summed, ("z", "xh", "c"), split_axis=0, concat_axis=0, tiled=True)
    finished = middle.astype(jnp.float32) + summed.reshape(128, 4096).astype(jnp.float32)
    return finished.astype(jnp.bfloat16).reshape(residual.shape)


def solution(mesh):
    split = Mesh(mesh.devices.reshape(SIZES), AXES)
    seq, head = ("z", "xh", "c"), ("y", "xl")
    in_specs = (
        P(head, None, seq, None),
        P(None, None, seq, head),
        P(None, None, seq, head),
        P(None, None, seq, head),
        P(head, seq),
        P(seq, head),
        P(seq, head),
        P(seq, head),
        P(head, seq),
    )
    out_specs = P(head, None, seq, None)
    return jax.shard_map(shards, mesh=split, in_specs=in_specs, out_specs=out_specs, check_vma=False)
```

```python
import numpy as np

import jax
import jax.numpy as jnp
from jax import lax
from jax.experimental import pallas as pl
from jax.experimental.pallas import tpu as pltpu
from jax.sharding import Mesh
from jax.sharding import PartitionSpec as P

HDIM = 128
AXES = ("z", "xh", "c", "y", "xl")
SIZES = (4, 2, 2, 4, 2)
RING = 4
SHORT = pl.CostEstimate(flops=1 << 20, bytes_accessed=1 << 16, transcendentals=0)
VMEM_LIMIT = 28 * 1024 * 1024


def permutation(move):
    pairs = []
    for source in range(int(np.prod(SIZES))):
        z, xh, c, y, xl = (int(v) for v in np.unravel_index(source, SIZES))
        z, x, c, y = (v % n for v, n in zip(move(z, 2 * xh + xl, c, y), (4, 4, 2, 4)))
        pairs.append((source, int(np.ravel_multi_index((z, x // 2, c, y, x % 2), SIZES))))
    return pairs


def from_y(array, d):
    return lax.ppermute(array, AXES, permutation(lambda z, x, c, y: (z, x, c, y - d)))


def to_y(array, d):
    return lax.ppermute(array, AXES, permutation(lambda z, x, c, y: (z, x, c, y + d)))


def swap_xl(array):
    return lax.ppermute(array, AXES, permutation(lambda z, x, c, y: (z, x ^ 1, c, y)))


def swap_core(array):
    return lax.ppermute(array, AXES, permutation(lambda z, x, c, y: (z, x, 1 - c, y)))


def from_first(array, d):
    return lax.ppermute(
        array, AXES, permutation(lambda z, x, c, y: (z - d * c, x - d * (1 - c), c, y))
    )


def from_second(array, d):
    return lax.ppermute(
        array, AXES, permutation(lambda z, x, c, y: (z - d * (1 - c), x - d * c, c, y))
    )


def after(array, *others):
    return lax.optimization_barrier((array,) + others)[0]


def ring_spots(coords, spots):
    z, x, c = coords[0], coords[1], coords[2]
    found = []
    for n, (j, first, count) in enumerate(spots):
        for k in range(count):
            i = first + k
            px = lax.rem(x + i + c * (j - i), RING)
            pz = lax.rem(z + j + c * (i - j), RING)
            found.append((n, k, pz * 2 + lax.div(px, 2), lax.rem(px, 2)))
    return found


def load(coords, pieces, shapes, copies_of, name, previous=()):
    count = len(shapes)

    def kernel(coords, *rest):
        refs, weights, sems = rest[: len(pieces)], rest[-1 - count : -1], rest[-1]
        copies = [
            pltpu.make_async_copy(source, target, sems.at[n])
            for n, (source, target) in enumerate(copies_of(coords, refs, weights))
        ]
        for copy in copies:
            copy.start()
        for copy in copies:
            copy.wait()

    in_vmem = pl.BlockSpec(memory_space=pltpu.VMEM)
    return pl.pallas_call(
        kernel,
        out_shape=[pltpu.VMEM(shape, jnp.bfloat16) for shape in shapes],
        in_specs=[pl.BlockSpec(memory_space=pltpu.SMEM)]
        + [pl.BlockSpec(memory_space=pltpu.HBM)] * len(pieces)
        + [in_vmem] * len(previous),
        out_specs=[in_vmem] * count,
        input_output_aliases={1 + len(pieces) + n: n for n in range(len(previous))},
        scratch_shapes=[pltpu.SemaphoreType.DMA((32 * count,))],
        compiler_params=pltpu.CompilerParams(vmem_limit_bytes=VMEM_LIMIT),
        cost_estimate=SHORT,
        name=name,
    )(
        coords,
        *[pltpu.with_memory_space_constraint(piece, pltpu.HBM) for piece in pieces],
        *[pltpu.with_memory_space_constraint(array, pltpu.VMEM) for array in previous],
    )


def load_temporal(coords, pieces, spots, previous=()):
    def copies(coords, refs, weights):
        for n, entry, zx, xl in ring_spots(coords, spots):
            for r in range(2):
                s = zx * 2 + coords[2] + r - 2 * r * coords[2]
                rows = pl.ds(pl.multiple_of(s * 256, 256), 256)
                for w, weight in enumerate(weights[:3]):
                    yield refs[n].at[entry, 4 * r + w], weight.at[xl, rows]
                yield refs[n].at[entry, 4 * r + 3], weights[3].at[s, xl]

    shapes = [(2, 4096, 256)] * 3 + [(16, 2, 256, 256)]
    return load(coords, pieces, shapes, copies, "load_temporal", previous)


def load_out(coords, pieces):
    spots = [(0, 0, 2), (0, 2, 2), (1, 0, 2), (3, 2, 2), (1, 2, 2), (3, 0, 2), (2, 0, 2), (2, 2, 2)]

    def copies(coords, refs, weights):
        for n, entry, zx, xl in ring_spots(coords, spots):
            yield refs[n].at[entry], weights[0].at[zx, pl.ds(xl * 2, 2)]

    return load(coords, pieces, [(8, 4, 256, 256)], copies, "load_out")[0]


def project_out(context, weight, outs):
    starts = np.cumsum([0] + [out.shape[0] for out in outs])

    def step(n, carry):
        part = jnp.dot(
            context[...], weight[n].reshape(-1, 256), preferred_element_type=jnp.float32
        ).astype(jnp.bfloat16)
        columns = pl.ds(pl.multiple_of(n * 256, 256), 256)
        for start, out in zip(starts, outs):
            out[:, columns] = part[start : start + out.shape[0]]
        return carry

    lax.fori_loop(0, weight.shape[0], step, 0)


def spatial_out_kernel(coords, *rest):
    sources, weight, outs, context = rest[:4], rest[4], rest[5:-1], rest[-1]
    y, xl = coords[3], coords[4]
    for d in range(RING):
        block = lax.rem(y + d, RING)
        for n, source in enumerate(sources):
            half = xl + (n % 2) * (1 - 2 * xl)
            columns = pl.ds(pl.multiple_of(half * 512, 512), 512)
            start = d * 256 + (n // 2) * 128
            context[start : start + 128, columns] = source[block]
    project_out(context, weight, outs)


def spatial_out_call(coords, sources, weight):
    in_vmem = pl.BlockSpec(memory_space=pltpu.VMEM)
    return pl.pallas_call(
        spatial_out_kernel,
        out_shape=[jax.ShapeDtypeStruct((256, 2048), jnp.bfloat16)] * RING,
        in_specs=[pl.BlockSpec(memory_space=pltpu.SMEM)] + [in_vmem] * 5,
        out_specs=[in_vmem] * RING,
        scratch_shapes=[pltpu.VMEM((1024, 1024), jnp.bfloat16)],
        compiler_params=pltpu.CompilerParams(vmem_limit_bytes=VMEM_LIMIT),
        cost_estimate=SHORT,
        name="spatial_out",
    )(coords, *sources, pltpu.with_memory_space_constraint(weight, pltpu.VMEM))


def temporal_call(blocks, weights):
    sizes = [block.shape[0] for block in blocks]
    total = sum(sizes)
    count = total // 128
    shapes = [(128, 4096)] * (count // 2) + [(64 * count, 4096)]

    def kernel(*rest):
        tokens, rest = rest[: len(sizes)], rest[len(sizes) :]
        weights, last, outs = rest[:3], rest[3], rest[4:-3]
        rows, projected, context = rest[-3:]
        start = 0
        for token, size in zip(tokens, sizes):
            rows[start : start + size] = token[...]
            start += size

        for w, weight in enumerate(weights):

            def project(n, carry, w=w, weight=weight):
                part = jnp.dot(rows[...], weight[n], preferred_element_type=jnp.float32)
                columns = pl.ds(pl.multiple_of(n * 256, 256), 256)
                projected[w, :, columns] = part.astype(jnp.bfloat16)
                return carry

            lax.fori_loop(0, 2, project, 0)
        video = lax.rem(lax.div(lax.broadcasted_iota(jnp.int32, (128, 128), 0), 2), 4)
        video_key = lax.rem(lax.div(lax.broadcasted_iota(jnp.int32, (128, 128), 1), 2), 4)
        same = video == video_key
        heads = [slice(h * HDIM, (h + 1) * HDIM) for h in range(4)]
        for b in range(count):
            at = slice(b * 128, (b + 1) * 128)
            scores = [
                lax.dot_general(
                    projected[0, at, h],
                    projected[1, at, h],
                    (((1,), (1,)), ((), ())),
                    preferred_element_type=jnp.float32,
                )
                for h in heads
            ]
            exponents = [jnp.where(same, jnp.exp(s * HDIM ** (-0.5)), 0.0) for s in scores]
            shares = [
                (e / jnp.sum(e, axis=-1, keepdims=True)).astype(jnp.bfloat16) for e in exponents
            ]
            for h, share in zip(heads, shares):
                context[at, h] = jnp.dot(
                    share, projected[2, at, h], preferred_element_type=jnp.float32
                ).astype(jnp.bfloat16)
        project_out(context, last, outs)

    in_vmem = pl.BlockSpec(memory_space=pltpu.VMEM)
    return pl.pallas_call(
        kernel,
        out_shape=[jax.ShapeDtypeStruct(shape, jnp.bfloat16) for shape in shapes],
        in_specs=[in_vmem] * (len(sizes) + 4),
        out_specs=[in_vmem] * len(shapes),
        scratch_shapes=[
            pltpu.VMEM((total, 4096), jnp.bfloat16),
            pltpu.VMEM((3, total, 512), jnp.bfloat16),
            pltpu.VMEM((total, 512), jnp.bfloat16),
        ],
        compiler_params=pltpu.CompilerParams(vmem_limit_bytes=VMEM_LIMIT),
        cost_estimate=SHORT,
        name="temporal",
    )(
        *blocks,
        *[pltpu.with_memory_space_constraint(w, pltpu.VMEM) for w in weights],
    )


def spatial_scores(queries, keys_in, values_in):
    shaped = [
        member.reshape(member.shape[:2] + (-1, HDIM)) for member in (queries, keys_in, values_in)
    ]
    scores = jnp.einsum(
        "ighc,jghc->ghij", shaped[0], shaped[1], preferred_element_type=jnp.float32
    ) * HDIM ** (-0.5)
    exponent = jnp.exp(scores)
    weights = (exponent / jnp.sum(exponent, axis=-1, keepdims=True)).astype(jnp.bfloat16)
    return weights, shaped[2]


def spatial_context(weights, values_in):
    context = jnp.einsum(
        "ghij,jghc->ighc", weights, values_in, preferred_element_type=jnp.float32
    )
    return context.astype(jnp.bfloat16)


def norm_call(coords, residual, mine, other):
    def kernel(coords, res, mine, other, middle, normed, total):
        c = coords[2]
        for n in range(8):
            for part, core in ((mine, c), (other, 1 - c)):
                columns = pl.ds(pl.multiple_of(n * 512 + core * 256, 256), 256)
                total[:, columns] = part[:, n * 256 : (n + 1) * 256]

        def step(n, carry):
            rows = pl.ds(pl.multiple_of(n * 16, 16), 16)
            summed = res[rows].astype(jnp.float32) + total[rows].astype(jnp.float32)
            rounded = summed.astype(jnp.bfloat16)
            middle[rows] = rounded
            values = rounded.astype(jnp.float32)
            centred = values - jnp.mean(values, axis=-1, keepdims=True)
            variance = jnp.mean(centred * centred, axis=-1, keepdims=True)
            normed[rows] = (centred * lax.rsqrt(variance + 1e-06)).astype(jnp.bfloat16)
            return carry

        lax.fori_loop(0, 8, step, 0)

    in_vmem = pl.BlockSpec(memory_space=pltpu.VMEM)
    rows = jax.ShapeDtypeStruct((128, 4096), jnp.bfloat16)
    return pl.pallas_call(
        kernel,
        out_shape=[rows, rows],
        in_specs=[pl.BlockSpec(memory_space=pltpu.SMEM)] + [in_vmem] * 3,
        out_specs=[in_vmem] * 2,
        scratch_shapes=[pltpu.VMEM((128, 4096), jnp.bfloat16)],
        compiler_params=pltpu.CompilerParams(vmem_limit_bytes=VMEM_LIMIT),
        cost_estimate=SHORT,
        name="norm",
    )(coords, residual, mine, other)


def shards(
    residual,
    spatial_query,
    spatial_key,
    spatial_value,
    spatial_out,
    temporal_query,
    temporal_key,
    temporal_value,
    temporal_out,
):
    z, xh, c, y, xl = (lax.axis_index(name) for name in AXES)
    coords = jnp.stack([z, 2 * xh + xl, c, y, xl]).astype(jnp.int32)

    layout = (128, 8, 512)
    scores, values_in = spatial_scores(
        *(array.reshape(layout) for array in (spatial_query, spatial_key, spatial_value))
    )

    context = spatial_context(scores, values_in).reshape(RING, 2, 128, 512)
    own, other = (
        lax.dynamic_index_in_dim(context, which, axis=1, keepdims=False) for which in (xl, 1 - xl)
    )

    out_shard = spatial_out.reshape(2, 256, 256)
    out_low = jnp.stack([out_shard, from_first(out_shard, 1)])
    out_high = jnp.stack([from_first(out_shard, 2), from_first(out_shard, -1)])
    out_low, out_high, own, other = lax.optimization_barrier((out_low, out_high, own, other))
    out_own = [out_low, out_high, from_second(out_low, 1), from_second(out_high, -1)]
    out_own += [from_second(out_high, 1), from_second(out_low, -1)]
    out_own += [from_second(out_own[2], 1), from_second(out_own[3], -1)]
    other = swap_xl(other)
    sources = [own, other, swap_core(own)]
    *sources, residual_rows = lax.optimization_barrier(
        (*sources, residual.reshape(128, 4096), *out_own)
    )
    sources, out_own, residual_rows = sources[:3], sources[4:] + [residual_rows], sources[3]
    sources.append(swap_core(sources[1]))
    tiles = jnp.stack(
        [w.reshape(256, 2, 256) for w in (temporal_query, temporal_key, temporal_value)]
        + [temporal_out.reshape(2, 256, 256).swapaxes(0, 1)]
    ).transpose(2, 0, 1, 3)
    mine, theirs = (
        lax.dynamic_index_in_dim(tiles, which, axis=0, keepdims=False) for which in (c, 1 - c)
    )
    shard = after(jnp.concatenate([mine, swap_core(theirs)]), *out_own[1:])
    shards_first = [shard] + [from_first(shard, d) for d in range(1, RING)]
    parts = spatial_out_call(coords, sources, load_out(coords, out_own))

    far = [to_y(parts[2][:128], 1), to_y(parts[2][128:], -1)]
    near_p = jnp.concatenate([parts[1][:128] + far[0], parts[1][128:]])
    near_m = jnp.concatenate([parts[3][:128], parts[3][128:] + far[1]])
    first = jnp.stack(lax.optimization_barrier((*shards_first, *far))[:RING])
    first, near_p, near_m = lax.optimization_barrier((first, near_p, near_m))
    pieces = [first, from_second(first, 1), from_second(first, -1)]
    total = parts[0].astype(jnp.float32)
    for part in (to_y(near_p, 1), to_y(near_m, -1)):
        total = total + part.astype(jnp.float32)
    total = total.astype(jnp.bfloat16)
    middle, normed = norm_call(coords, residual_rows, total[:128], swap_core(total[128:]))
    normed = lax.all_to_all(
        normed.reshape(16, 8, 4096), ("z", "xh", "c"), split_axis=0, concat_axis=0, tiled=True
    ).reshape(128, 4096)
    normed, *pieces = lax.optimization_barrier((normed, *pieces))
    next_p, next_m = from_y(normed, 1), from_y(normed, -1)
    last = [from_second(pieces[1][:2], 1), from_second(pieces[2][2:], -1)]
    weights = load_temporal(coords, pieces, [(j, 0, RING) for j in (0, 1, 3)])
    *last, next_p, next_m, w_0, w_1, w_2, w_3 = lax.optimization_barrier(
        (*last, next_p, next_m, *weights)
    )
    weights = [w_0, w_1, w_2, w_3]
    weights = load_temporal(coords, last, [(2, 0, 2), (2, 2, 2)], weights)

    far = [from_y(next_p[:64], 1), from_y(next_m[64:], -1)]
    near = [next_p, next_m, swap_core(next_p), swap_core(next_m)]
    *near, own_swapped = lax.optimization_barrier((*near, swap_core(normed)))

    part_p, part_m, others = temporal_call(near, weights)
    *far, part_p, part_m, others = lax.optimization_barrier((*far, part_p, part_m, others))
    far += [swap_core(half) for half in far]
    *far, others = lax.optimization_barrier((*far, others))
    others = swap_core(others)
    part, far_others = temporal_call(far, weights)
    far_others, others = lax.optimization_barrier((far_others, others))
    part = (part.astype(jnp.float32) + swap_core(far_others).astype(jnp.float32)).astype(jnp.bfloat16)
    far = [to_y(part[:64], 1), to_y(part[64:], -1)]
    own, own_others = temporal_call([normed, own_swapped], weights)
    *far, own, own_others = lax.optimization_barrier((*far, own, own_others))
    total = own.astype(jnp.float32) + swap_core(own_others).astype(jnp.float32)
    zeros = jnp.zeros((64, 4096), jnp.bfloat16)
    for d, part, other, passed in (
        (1, part_p, others[:128], [far[0], zeros]),
        (-1, part_m, others[128:], [zeros, far[1]]),
    ):
        part = part.astype(jnp.float32) + other.astype(jnp.float32)
        part = (part + jnp.concatenate(passed).astype(jnp.float32)).astype(jnp.bfloat16)
        total = total + to_y(part, d).astype(jnp.float32)
    summed = total.astype(jnp.bfloat16).reshape(16, 8, 4096)
    summed = lax.all_to_all(summed, ("z", "xh", "c"), split_axis=0, concat_axis=0, tiled=True)
    finished = middle.astype(jnp.float32) + summed.reshape(128, 4096).astype(jnp.float32)
    return finished.astype(jnp.bfloat16).reshape(residual.shape)


def solution(mesh):
    split = Mesh(mesh.devices.reshape(SIZES), AXES)
    seq, head = ("z", "xh", "c"), ("y", "xl")
    in_specs = (
        P(head, None, seq, None),
        P(None, None, seq, head),
        P(None, None, seq, head),
        P(None, None, seq, head),
        P(head, seq),
        P(seq, head),
        P(seq, head),
        P(seq, head),
        P(head, seq),
    )
    out_specs = P(head, None, seq, None)
    return jax.shard_map(shards, mesh=split, in_specs=in_specs, out_specs=out_specs, check_vma=False)
```

```python
import numpy as np

import jax
import jax.numpy as jnp
from jax import lax
from jax.experimental import pallas as pl
from jax.experimental.pallas import tpu as pltpu
from jax.sharding import Mesh
from jax.sharding import PartitionSpec as P

HDIM = 128
AXES = ("z", "xh", "c", "y", "xl")
SIZES = (4, 2, 2, 4, 2)
RING = 4
SHORT = pl.CostEstimate(flops=1 << 20, bytes_accessed=1 << 16, transcendentals=0)
VMEM_LIMIT = 28 * 1024 * 1024


def permutation(move):
    pairs = []
    for source in range(int(np.prod(SIZES))):
        z, xh, c, y, xl = (int(v) for v in np.unravel_index(source, SIZES))
        z, x, c, y = (v % n for v, n in zip(move(z, 2 * xh + xl, c, y), (4, 4, 2, 4)))
        pairs.append((source, int(np.ravel_multi_index((z, x // 2, c, y, x % 2), SIZES))))
    return pairs


def from_y(array, d):
    return lax.ppermute(array, AXES, permutation(lambda z, x, c, y: (z, x, c, y - d)))


def to_y(array, d):
    return lax.ppermute(array, AXES, permutation(lambda z, x, c, y: (z, x, c, y + d)))


def swap_xl(array):
    return lax.ppermute(array, AXES, permutation(lambda z, x, c, y: (z, x ^ 1, c, y)))


def swap_core(array):
    return lax.ppermute(array, AXES, permutation(lambda z, x, c, y: (z, x, 1 - c, y)))


def from_first(array, d):
    return lax.ppermute(
        array, AXES, permutation(lambda z, x, c, y: (z - d * c, x - d * (1 - c), c, y))
    )


def from_second(array, d):
    return lax.ppermute(
        array, AXES, permutation(lambda z, x, c, y: (z - d * (1 - c), x - d * c, c, y))
    )


def after(array, *others):
    return lax.optimization_barrier((array,) + others)[0]


def ring_spots(coords, spots):
    z, x, c = coords[0], coords[1], coords[2]
    found = []
    for n, (j, first, count) in enumerate(spots):
        for k in range(count):
            i = first + k
            px = lax.rem(x + i + c * (j - i), RING)
            pz = lax.rem(z + j + c * (i - j), RING)
            found.append((n, k, pz * 2 + lax.div(px, 2), lax.rem(px, 2)))
    return found


def load(coords, pieces, shapes, copies_of, name, previous=()):
    count = len(shapes)

    def kernel(coords, *rest):
        refs, weights, sems = rest[: len(pieces)], rest[-1 - count : -1], rest[-1]
        copies = [
            pltpu.make_async_copy(source, target, sems.at[n])
            for n, (source, target) in enumerate(copies_of(coords, refs, weights))
        ]
        for copy in copies:
            copy.start()
        for copy in copies:
            copy.wait()

    in_vmem = pl.BlockSpec(memory_space=pltpu.VMEM)
    return pl.pallas_call(
        kernel,
        out_shape=[pltpu.VMEM(shape, jnp.bfloat16) for shape in shapes],
        in_specs=[pl.BlockSpec(memory_space=pltpu.SMEM)]
        + [pl.BlockSpec(memory_space=pltpu.HBM)] * len(pieces)
        + [in_vmem] * len(previous),
        out_specs=[in_vmem] * count,
        input_output_aliases={1 + len(pieces) + n: n for n in range(len(previous))},
        scratch_shapes=[pltpu.SemaphoreType.DMA((32 * count,))],
        compiler_params=pltpu.CompilerParams(vmem_limit_bytes=VMEM_LIMIT),
        cost_estimate=SHORT,
        name=name,
    )(
        coords,
        *[pltpu.with_memory_space_constraint(piece, pltpu.HBM) for piece in pieces],
        *[pltpu.with_memory_space_constraint(array, pltpu.VMEM) for array in previous],
    )


def load_temporal(coords, pieces, spots, previous=()):
    def copies(coords, refs, weights):
        for n, entry, zx, xl in ring_spots(coords, spots):
            for r in range(2):
                s = zx * 2 + coords[2] + r - 2 * r * coords[2]
                rows = pl.ds(pl.multiple_of(s * 256, 256), 256)
                for w, weight in enumerate(weights[:3]):
                    yield refs[n].at[entry, 4 * r + w], weight.at[xl, rows]
                yield refs[n].at[entry, 4 * r + 3], weights[3].at[s, xl]

    shapes = [(2, 4096, 256)] * 3 + [(16, 2, 256, 256)]
    return load(coords, pieces, shapes, copies, "load_temporal", previous)


def load_out(coords, pieces):
    spots = [(0, 0, 2), (0, 2, 2), (1, 0, 2), (3, 2, 2), (1, 2, 2), (3, 0, 2), (2, 0, 2), (2, 2, 2)]

    def copies(coords, refs, weights):
        for n, entry, zx, xl in ring_spots(coords, spots):
            yield refs[n].at[entry], weights[0].at[zx, pl.ds(xl * 2, 2)]

    return load(coords, pieces, [(8, 4, 256, 256)], copies, "load_out")[0]


def project_out(context, weight, outs):
    starts = np.cumsum([0] + [out.shape[0] for out in outs])

    def step(m, carry):
        for n in (4 * m, 4 * m + 1, 4 * m + 2, 4 * m + 3):
            part = jnp.dot(
                context[...], weight[n].reshape(-1, 256), preferred_element_type=jnp.float32
            ).astype(jnp.bfloat16)
            columns = pl.ds(pl.multiple_of(n * 256, 256), 256)
            for start, out in zip(starts, outs):
                out[:, columns] = part[start : start + out.shape[0]]
        return carry

    lax.fori_loop(0, weight.shape[0] // 4, step, 0)


def spatial_out_kernel(coords, *rest):
    sources, weight, outs, context = rest[:4], rest[4], rest[5:-1], rest[-1]
    y, xl = coords[3], coords[4]
    for d in range(RING):
        block = lax.rem(y + d, RING)
        for n, source in enumerate(sources):
            half = xl + (n % 2) * (1 - 2 * xl)
            columns = pl.ds(pl.multiple_of(half * 512, 512), 512)
            start = d * 256 + (n // 2) * 128
            context[start : start + 128, columns] = source[block]
    project_out(context, weight, outs)


def spatial_out_call(coords, sources, weight):
    in_vmem = pl.BlockSpec(memory_space=pltpu.VMEM)
    return pl.pallas_call(
        spatial_out_kernel,
        out_shape=[jax.ShapeDtypeStruct((256, 2048), jnp.bfloat16)] * RING,
        in_specs=[pl.BlockSpec(memory_space=pltpu.SMEM)] + [in_vmem] * 5,
        out_specs=[in_vmem] * RING,
        scratch_shapes=[pltpu.VMEM((1024, 1024), jnp.bfloat16)],
        compiler_params=pltpu.CompilerParams(vmem_limit_bytes=VMEM_LIMIT),
        cost_estimate=SHORT,
        name="spatial_out",
    )(coords, *sources, pltpu.with_memory_space_constraint(weight, pltpu.VMEM))


def temporal_call(blocks, weights):
    sizes = [block.shape[0] for block in blocks]
    total = sum(sizes)
    count = total // 128
    shapes = [(128, 4096)] * (count // 2) + [(64 * count, 4096)]

    def kernel(*rest):
        tokens, rest = rest[: len(sizes)], rest[len(sizes) :]
        weights, last, outs = rest[:3], rest[3], rest[4:-3]
        rows, projected, context = rest[-3:]
        start = 0
        for token, size in zip(tokens, sizes):
            rows[start : start + size] = token[...]
            start += size

        for w, weight in enumerate(weights):
            for n in range(2):
                part = jnp.dot(rows[...], weight[n], preferred_element_type=jnp.float32)
                projected[w, :, n * 256 : (n + 1) * 256] = part.astype(jnp.bfloat16)

        video = lax.rem(lax.div(lax.broadcasted_iota(jnp.int32, (128, 128), 0), 2), 4)
        video_key = lax.rem(lax.div(lax.broadcasted_iota(jnp.int32, (128, 128), 1), 2), 4)
        same = video == video_key
        heads = [slice(h * HDIM, (h + 1) * HDIM) for h in range(4)]
        for b in range(count):
            at = slice(b * 128, (b + 1) * 128)
            scores = [
                lax.dot_general(
                    projected[0, at, h],
                    projected[1, at, h],
                    (((1,), (1,)), ((), ())),
                    preferred_element_type=jnp.float32,
                )
                for h in heads
            ]
            exponents = [jnp.where(same, jnp.exp(s * HDIM ** (-0.5)), 0.0) for s in scores]
            shares = [
                (e / jnp.sum(e, axis=-1, keepdims=True)).astype(jnp.bfloat16) for e in exponents
            ]
            for h, share in zip(heads, shares):
                context[at, h] = jnp.dot(
                    share, projected[2, at, h], preferred_element_type=jnp.float32
                ).astype(jnp.bfloat16)
        project_out(context, last, outs)

    in_vmem = pl.BlockSpec(memory_space=pltpu.VMEM)
    return pl.pallas_call(
        kernel,
        out_shape=[jax.ShapeDtypeStruct(shape, jnp.bfloat16) for shape in shapes],
        in_specs=[in_vmem] * (len(sizes) + 4),
        out_specs=[in_vmem] * len(shapes),
        scratch_shapes=[
            pltpu.VMEM((total, 4096), jnp.bfloat16),
            pltpu.VMEM((3, total, 512), jnp.bfloat16),
            pltpu.VMEM((total, 512), jnp.bfloat16),
        ],
        compiler_params=pltpu.CompilerParams(vmem_limit_bytes=VMEM_LIMIT),
        cost_estimate=SHORT,
        name="temporal",
    )(
        *blocks,
        *[pltpu.with_memory_space_constraint(w, pltpu.VMEM) for w in weights],
    )


def spatial_scores(queries, keys_in, values_in):
    shaped = [
        member.reshape(member.shape[:2] + (-1, HDIM)) for member in (queries, keys_in, values_in)
    ]
    scores = jnp.einsum(
        "ighc,jghc->ghij", shaped[0], shaped[1], preferred_element_type=jnp.float32
    ) * HDIM ** (-0.5)
    exponent = jnp.exp(scores)
    weights = (exponent / jnp.sum(exponent, axis=-1, keepdims=True)).astype(jnp.bfloat16)
    return weights, shaped[2]


def spatial_context(weights, values_in):
    context = jnp.einsum(
        "ghij,jghc->ighc", weights, values_in, preferred_element_type=jnp.float32
    )
    return context.astype(jnp.bfloat16)


def norm_call(coords, residual, mine, other):
    def kernel(coords, res, mine, other, middle, normed, total):
        c = coords[2]
        for n in range(8):
            for part, core in ((mine, c), (other, 1 - c)):
                columns = pl.ds(pl.multiple_of(n * 512 + core * 256, 256), 256)
                total[:, columns] = part[:, n * 256 : (n + 1) * 256]

        def step(n, carry):
            rows = pl.ds(pl.multiple_of(n * 16, 16), 16)
            summed = res[rows].astype(jnp.float32) + total[rows].astype(jnp.float32)
            rounded = summed.astype(jnp.bfloat16)
            middle[rows] = rounded
            values = rounded.astype(jnp.float32)
            centred = values - jnp.mean(values, axis=-1, keepdims=True)
            variance = jnp.mean(centred * centred, axis=-1, keepdims=True)
            normed[rows] = (centred * lax.rsqrt(variance + 1e-06)).astype(jnp.bfloat16)
            return carry

        lax.fori_loop(0, 8, step, 0)

    in_vmem = pl.BlockSpec(memory_space=pltpu.VMEM)
    rows = jax.ShapeDtypeStruct((128, 4096), jnp.bfloat16)
    return pl.pallas_call(
        kernel,
        out_shape=[rows, rows],
        in_specs=[pl.BlockSpec(memory_space=pltpu.SMEM)] + [in_vmem] * 3,
        out_specs=[in_vmem] * 2,
        scratch_shapes=[pltpu.VMEM((128, 4096), jnp.bfloat16)],
        compiler_params=pltpu.CompilerParams(vmem_limit_bytes=VMEM_LIMIT),
        cost_estimate=SHORT,
        name="norm",
    )(coords, residual, mine, other)


def shards(
    residual,
    spatial_query,
    spatial_key,
    spatial_value,
    spatial_out,
    temporal_query,
    temporal_key,
    temporal_value,
    temporal_out,
):
    z, xh, c, y, xl = (lax.axis_index(name) for name in AXES)
    coords = jnp.stack([z, 2 * xh + xl, c, y, xl]).astype(jnp.int32)

    layout = (128, 8, 512)
    scores, values_in = spatial_scores(
        *(array.reshape(layout) for array in (spatial_query, spatial_key, spatial_value))
    )

    context = spatial_context(scores, values_in).reshape(RING, 2, 128, 512)
    own, other = (
        lax.dynamic_index_in_dim(context, which, axis=1, keepdims=False) for which in (xl, 1 - xl)
    )

    out_shard = spatial_out.reshape(2, 256, 256)
    out_low = jnp.stack([out_shard, from_first(out_shard, 1)])
    out_high = jnp.stack([from_first(out_shard, 2), from_first(out_shard, -1)])
    out_low, out_high, own, other = lax.optimization_barrier((out_low, out_high, own, other))
    out_own = [out_low, out_high, from_second(out_low, 1), from_second(out_high, -1)]
    out_own += [from_second(out_high, 1), from_second(out_low, -1)]
    out_own += [from_second(out_own[2], 1), from_second(out_own[3], -1)]
    other = swap_xl(other)
    sources = [own, other, swap_core(own)]
    *sources, residual_rows = lax.optimization_barrier(
        (*sources, residual.reshape(128, 4096), *out_own)
    )
    sources, out_own, residual_rows = sources[:3], sources[4:] + [residual_rows], sources[3]
    sources.append(swap_core(sources[1]))
    tiles = jnp.stack(
        [w.reshape(256, 2, 256) for w in (temporal_query, temporal_key, temporal_value)]
        + [temporal_out.reshape(2, 256, 256).swapaxes(0, 1)]
    ).transpose(2, 0, 1, 3)
    mine, theirs = (
        lax.dynamic_index_in_dim(tiles, which, axis=0, keepdims=False) for which in (c, 1 - c)
    )
    shard = after(jnp.concatenate([mine, swap_core(theirs)]), *out_own[1:])
    shards_first = [shard] + [from_first(shard, d) for d in range(1, RING)]
    parts = spatial_out_call(coords, sources, load_out(coords, out_own))

    far = [to_y(parts[2][:128], 1), to_y(parts[2][128:], -1)]
    near_p = jnp.concatenate([parts[1][:128] + far[0], parts[1][128:]])
    near_m = jnp.concatenate([parts[3][:128], parts[3][128:] + far[1]])
    first = jnp.stack(lax.optimization_barrier((*shards_first, *far))[:RING])
    first, near_p, near_m = lax.optimization_barrier((first, near_p, near_m))
    pieces = [first, from_second(first, 1), from_second(first, -1)]
    total = parts[0].astype(jnp.float32)
    for part in (to_y(near_p, 1), to_y(near_m, -1)):
        total = total + part.astype(jnp.float32)
    total = total.astype(jnp.bfloat16)
    middle, normed = norm_call(coords, residual_rows, total[:128], swap_core(total[128:]))
    normed = lax.all_to_all(
        normed.reshape(16, 8, 4096), ("z", "xh", "c"), split_axis=0, concat_axis=0, tiled=True
    ).reshape(128, 4096)
    normed, *pieces = lax.optimization_barrier((normed, *pieces))
    next_p, next_m = from_y(normed, 1), from_y(normed, -1)
    last = [from_second(pieces[1][:2], 1), from_second(pieces[2][2:], -1)]
    weights = load_temporal(coords, pieces, [(j, 0, RING) for j in (0, 1, 3)])
    *last, next_p, next_m, w_0, w_1, w_2, w_3 = lax.optimization_barrier(
        (*last, next_p, next_m, *weights)
    )
    weights = [w_0, w_1, w_2, w_3]
    weights = load_temporal(coords, last, [(2, 0, 2), (2, 2, 2)], weights)

    far = [from_y(next_p[:64], 1), from_y(next_m[64:], -1)]
    near = [next_p, next_m, swap_core(next_p), swap_core(next_m)]
    *near, own_swapped = lax.optimization_barrier((*near, swap_core(normed)))

    part_p, part_m, others = temporal_call(near, weights)
    *far, part_p, part_m, others = lax.optimization_barrier((*far, part_p, part_m, others))
    far += [swap_core(half) for half in far]
    *far, others = lax.optimization_barrier((*far, others))
    others = swap_core(others)
    part, far_others = temporal_call(far, weights)
    far_others, others = lax.optimization_barrier((far_others, others))
    part = (part.astype(jnp.float32) + swap_core(far_others).astype(jnp.float32)).astype(jnp.bfloat16)
    far = [to_y(part[:64], 1), to_y(part[64:], -1)]
    own, own_others = temporal_call([normed, own_swapped], weights)
    *far, own, own_others = lax.optimization_barrier((*far, own, own_others))
    total = own.astype(jnp.float32) + swap_core(own_others).astype(jnp.float32)
    zeros = jnp.zeros((64, 4096), jnp.bfloat16)
    for d, part, other, passed in (
        (1, part_p, others[:128], [far[0], zeros]),
        (-1, part_m, others[128:], [zeros, far[1]]),
    ):
        part = part.astype(jnp.float32) + other.astype(jnp.float32)
        part = (part + jnp.concatenate(passed).astype(jnp.float32)).astype(jnp.bfloat16)
        total = total + to_y(part, d).astype(jnp.float32)
    summed = total.astype(jnp.bfloat16).reshape(16, 8, 4096)
    summed = lax.all_to_all(summed, ("z", "xh", "c"), split_axis=0, concat_axis=0, tiled=True)
    finished = middle.astype(jnp.float32) + summed.reshape(128, 4096).astype(jnp.float32)
    return finished.astype(jnp.bfloat16).reshape(residual.shape)


def solution(mesh):
    split = Mesh(mesh.devices.reshape(SIZES), AXES)
    seq, head = ("z", "xh", "c"), ("y", "xl")
    in_specs = (
        P(head, None, seq, None),
        P(None, None, seq, head),
        P(None, None, seq, head),
        P(None, None, seq, head),
        P(head, seq),
        P(seq, head),
        P(seq, head),
        P(seq, head),
        P(head, seq),
    )
    out_specs = P(head, None, seq, None)
    return jax.shard_map(shards, mesh=split, in_specs=in_specs, out_specs=out_specs, check_vma=False)
```

```python
import numpy as np

import jax
import jax.numpy as jnp
from jax import lax
from jax.experimental import pallas as pl
from jax.experimental.pallas import tpu as pltpu
from jax.sharding import Mesh
from jax.sharding import PartitionSpec as P

HDIM = 128
AXES = ("z", "xh", "c", "y", "xl")
SIZES = (4, 2, 2, 4, 2)
RING = 4
SHORT = pl.CostEstimate(flops=1 << 20, bytes_accessed=1 << 16, transcendentals=0)
VMEM_LIMIT = 28 * 1024 * 1024


def permutation(move):
    pairs = []
    for source in range(int(np.prod(SIZES))):
        z, xh, c, y, xl = (int(v) for v in np.unravel_index(source, SIZES))
        z, x, c, y = (v % n for v, n in zip(move(z, 2 * xh + xl, c, y), (4, 4, 2, 4)))
        pairs.append((source, int(np.ravel_multi_index((z, x // 2, c, y, x % 2), SIZES))))
    return pairs


def from_y(array, d):
    return lax.ppermute(array, AXES, permutation(lambda z, x, c, y: (z, x, c, y - d)))


def to_y(array, d):
    return lax.ppermute(array, AXES, permutation(lambda z, x, c, y: (z, x, c, y + d)))


def swap_xl(array):
    return lax.ppermute(array, AXES, permutation(lambda z, x, c, y: (z, x ^ 1, c, y)))


def swap_core(array):
    return lax.ppermute(array, AXES, permutation(lambda z, x, c, y: (z, x, 1 - c, y)))


def from_first(array, d):
    return lax.ppermute(
        array, AXES, permutation(lambda z, x, c, y: (z - d * c, x - d * (1 - c), c, y))
    )


def from_second(array, d):
    return lax.ppermute(
        array, AXES, permutation(lambda z, x, c, y: (z - d * (1 - c), x - d * c, c, y))
    )


def after(array, *others):
    return lax.optimization_barrier((array,) + others)[0]


def ring_spots(coords, spots):
    z, x, c = coords[0], coords[1], coords[2]
    found = []
    for n, (j, first, count) in enumerate(spots):
        for k in range(count):
            i = first + k
            px = lax.rem(x + i + c * (j - i), RING)
            pz = lax.rem(z + j + c * (i - j), RING)
            found.append((n, k, pz * 2 + lax.div(px, 2), lax.rem(px, 2)))
    return found


def load(coords, pieces, shapes, copies_of, name, previous=()):
    count = len(shapes)

    def kernel(coords, *rest):
        refs, weights, sems = rest[: len(pieces)], rest[-1 - count : -1], rest[-1]
        copies = [
            pltpu.make_async_copy(source, target, sems.at[n])
            for n, (source, target) in enumerate(copies_of(coords, refs, weights))
        ]
        for copy in copies:
            copy.start()
        for copy in copies:
            copy.wait()

    in_vmem = pl.BlockSpec(memory_space=pltpu.VMEM)
    return pl.pallas_call(
        kernel,
        out_shape=[pltpu.VMEM(shape, jnp.bfloat16) for shape in shapes],
        in_specs=[pl.BlockSpec(memory_space=pltpu.SMEM)]
        + [pl.BlockSpec(memory_space=pltpu.HBM)] * len(pieces)
        + [in_vmem] * len(previous),
        out_specs=[in_vmem] * count,
        input_output_aliases={1 + len(pieces) + n: n for n in range(len(previous))},
        scratch_shapes=[pltpu.SemaphoreType.DMA((32 * count,))],
        compiler_params=pltpu.CompilerParams(vmem_limit_bytes=VMEM_LIMIT),
        cost_estimate=SHORT,
        name=name,
    )(
        coords,
        *[pltpu.with_memory_space_constraint(piece, pltpu.HBM) for piece in pieces],
        *[pltpu.with_memory_space_constraint(array, pltpu.VMEM) for array in previous],
    )


def load_temporal(coords, pieces, spots, previous=()):
    def copies(coords, refs, weights):
        for n, entry, zx, xl in ring_spots(coords, spots):
            for r in range(2):
                s = zx * 2 + coords[2] + r - 2 * r * coords[2]
                rows = pl.ds(pl.multiple_of(s * 256, 256), 256)
                for w, weight in enumerate(weights[:3]):
                    yield refs[n].at[entry, 4 * r + w], weight.at[xl, rows]
                yield refs[n].at[entry, 4 * r + 3], weights[3].at[s, xl]

    shapes = [(2, 4096, 256)] * 3 + [(16, 2, 256, 256)]
    return load(coords, pieces, shapes, copies, "load_temporal", previous)


def load_out(coords, pieces):
    spots = [(0, 0, 2), (0, 2, 2), (1, 0, 2), (3, 2, 2), (1, 2, 2), (3, 0, 2), (2, 0, 2), (2, 2, 2)]

    def copies(coords, refs, weights):
        for n, entry, zx, xl in ring_spots(coords, spots):
            yield refs[n].at[entry], weights[0].at[zx, pl.ds(xl * 2, 2)]

    return load(coords, pieces, [(8, 4, 256, 256)], copies, "load_out")[0]


def project_out(context, weight, outs):
    starts = np.cumsum([0] + [out.shape[0] for out in outs])

    def step(m, carry):
        for n in (4 * m, 4 * m + 1, 4 * m + 2, 4 * m + 3):
            part = jnp.dot(
                context[...], weight[n].reshape(-1, 256), preferred_element_type=jnp.float32
            ).astype(jnp.bfloat16)
            columns = pl.ds(pl.multiple_of(n * 256, 256), 256)
            for start, out in zip(starts, outs):
                out[:, columns] = part[start : start + out.shape[0]]
        return carry

    lax.fori_loop(0, weight.shape[0] // 4, step, 0)


def spatial_out_kernel(coords, *rest):
    sources, weight, outs, context = rest[:4], rest[4], rest[5:-1], rest[-1]
    y, xl = coords[3], coords[4]
    for d in range(RING):
        block = lax.rem(y + d, RING)
        for n, source in enumerate(sources):
            half = xl + (n % 2) * (1 - 2 * xl)
            columns = pl.ds(pl.multiple_of(half * 512, 512), 512)
            start = d * 256 + (n // 2) * 128
            context[start : start + 128, columns] = source[block]
    project_out(context, weight, outs)


def spatial_out_call(coords, sources, weight):
    in_vmem = pl.BlockSpec(memory_space=pltpu.VMEM)
    return pl.pallas_call(
        spatial_out_kernel,
        out_shape=[jax.ShapeDtypeStruct((256, 2048), jnp.bfloat16)] * RING,
        in_specs=[pl.BlockSpec(memory_space=pltpu.SMEM)] + [in_vmem] * 5,
        out_specs=[in_vmem] * RING,
        scratch_shapes=[pltpu.VMEM((1024, 1024), jnp.bfloat16)],
        compiler_params=pltpu.CompilerParams(vmem_limit_bytes=VMEM_LIMIT),
        cost_estimate=SHORT,
        name="spatial_out",
    )(coords, *sources, pltpu.with_memory_space_constraint(weight, pltpu.VMEM))


def temporal_call(blocks, weights):
    sizes = [block.shape[0] for block in blocks]
    total = sum(sizes)
    count = total // 128
    shapes = [(128, 4096)] * (count // 2) + [(64 * count, 4096)]

    def kernel(*rest):
        tokens, rest = rest[: len(sizes)], rest[len(sizes) :]
        weights, last, outs = rest[:3], rest[3], rest[4:-3]
        rows, projected, context = rest[-3:]
        start = 0
        for token, size in zip(tokens, sizes):
            rows[start : start + size] = token[...]
            start += size

        for w, weight in enumerate(weights):
            for n in range(2):
                part = jnp.dot(rows[...], weight[n], preferred_element_type=jnp.float32)
                projected[w, :, n * 256 : (n + 1) * 256] = part.astype(jnp.bfloat16)

        video = lax.rem(lax.div(lax.broadcasted_iota(jnp.int32, (128, 128), 0), 2), 4)
        video_key = lax.rem(lax.div(lax.broadcasted_iota(jnp.int32, (128, 128), 1), 2), 4)
        same = video == video_key
        heads = [slice(h * HDIM, (h + 1) * HDIM) for h in range(4)]
        for b in range(count):
            at = slice(b * 128, (b + 1) * 128)
            scores = [
                lax.dot_general(
                    projected[0, at, h],
                    projected[1, at, h],
                    (((1,), (1,)), ((), ())),
                    preferred_element_type=jnp.float32,
                )
                for h in heads
            ]
            exponents = [jnp.where(same, jnp.exp(s * HDIM ** (-0.5)), 0.0) for s in scores]
            shares = [
                (e / jnp.sum(e, axis=-1, keepdims=True)).astype(jnp.bfloat16) for e in exponents
            ]
            for h, share in zip(heads, shares):
                context[at, h] = jnp.dot(
                    share, projected[2, at, h], preferred_element_type=jnp.float32
                ).astype(jnp.bfloat16)
        project_out(context, last, outs)

    in_vmem = pl.BlockSpec(memory_space=pltpu.VMEM)
    return pl.pallas_call(
        kernel,
        out_shape=[jax.ShapeDtypeStruct(shape, jnp.bfloat16) for shape in shapes],
        in_specs=[in_vmem] * (len(sizes) + 4),
        out_specs=[in_vmem] * len(shapes),
        scratch_shapes=[
            pltpu.VMEM((total, 4096), jnp.bfloat16),
            pltpu.VMEM((3, total, 512), jnp.bfloat16),
            pltpu.VMEM((total, 512), jnp.bfloat16),
        ],
        compiler_params=pltpu.CompilerParams(vmem_limit_bytes=VMEM_LIMIT),
        cost_estimate=SHORT,
        name="temporal",
    )(
        *blocks,
        *[pltpu.with_memory_space_constraint(w, pltpu.VMEM) for w in weights],
    )


def spatial_scores(queries, keys_in, values_in):
    shaped = [
        member.reshape(member.shape[:2] + (-1, HDIM)) for member in (queries, keys_in, values_in)
    ]
    scores = jnp.einsum(
        "ighc,jghc->ghij", shaped[0], shaped[1], preferred_element_type=jnp.float32
    ) * HDIM ** (-0.5)
    exponent = jnp.exp(scores)
    weights = (exponent / jnp.sum(exponent, axis=-1, keepdims=True)).astype(jnp.bfloat16)
    return weights, shaped[2]


def spatial_context(weights, values_in):
    context = jnp.einsum(
        "ghij,jghc->ighc", weights, values_in, preferred_element_type=jnp.float32
    )
    return context.astype(jnp.bfloat16)


def norm_call(coords, residual, mine, other):
    def kernel(coords, res, mine, other, middle, normed, total):
        c = coords[2]
        for n in range(8):
            for part, core in ((mine, c), (other, 1 - c)):
                columns = pl.ds(pl.multiple_of(n * 512 + core * 256, 256), 256)
                total[:, columns] = part[:, n * 256 : (n + 1) * 256]

        def step(m, carry):
            for n in (2 * m, 2 * m + 1):
                rows = pl.ds(pl.multiple_of(n * 16, 16), 16)
                summed = res[rows].astype(jnp.float32) + total[rows].astype(jnp.float32)
                rounded = summed.astype(jnp.bfloat16)
                middle[rows] = rounded
                values = rounded.astype(jnp.float32)
                centred = values - jnp.mean(values, axis=-1, keepdims=True)
                variance = jnp.mean(centred * centred, axis=-1, keepdims=True)
                normed[rows] = (centred * lax.rsqrt(variance + 1e-06)).astype(jnp.bfloat16)
            return carry

        lax.fori_loop(0, 4, step, 0)

    in_vmem = pl.BlockSpec(memory_space=pltpu.VMEM)
    rows = jax.ShapeDtypeStruct((128, 4096), jnp.bfloat16)
    return pl.pallas_call(
        kernel,
        out_shape=[rows, rows],
        in_specs=[pl.BlockSpec(memory_space=pltpu.SMEM)] + [in_vmem] * 3,
        out_specs=[in_vmem] * 2,
        scratch_shapes=[pltpu.VMEM((128, 4096), jnp.bfloat16)],
        compiler_params=pltpu.CompilerParams(vmem_limit_bytes=VMEM_LIMIT),
        cost_estimate=SHORT,
        name="norm",
    )(coords, residual, mine, other)


def shards(
    residual,
    spatial_query,
    spatial_key,
    spatial_value,
    spatial_out,
    temporal_query,
    temporal_key,
    temporal_value,
    temporal_out,
):
    z, xh, c, y, xl = (lax.axis_index(name) for name in AXES)
    coords = jnp.stack([z, 2 * xh + xl, c, y, xl]).astype(jnp.int32)

    layout = (128, 8, 512)
    scores, values_in = spatial_scores(
        *(array.reshape(layout) for array in (spatial_query, spatial_key, spatial_value))
    )

    context = spatial_context(scores, values_in).reshape(RING, 2, 128, 512)
    own, other = (
        lax.dynamic_index_in_dim(context, which, axis=1, keepdims=False) for which in (xl, 1 - xl)
    )

    out_shard = spatial_out.reshape(2, 256, 256)
    out_low = jnp.stack([out_shard, from_first(out_shard, 1)])
    out_high = jnp.stack([from_first(out_shard, 2), from_first(out_shard, -1)])
    out_low, out_high, own, other = lax.optimization_barrier((out_low, out_high, own, other))
    out_own = [out_low, out_high, from_second(out_low, 1), from_second(out_high, -1)]
    out_own += [from_second(out_high, 1), from_second(out_low, -1)]
    out_own += [from_second(out_own[2], 1), from_second(out_own[3], -1)]
    other = swap_xl(other)
    sources = [own, other, swap_core(own)]
    *sources, residual_rows = lax.optimization_barrier(
        (*sources, residual.reshape(128, 4096), *out_own)
    )
    sources, out_own, residual_rows = sources[:3], sources[4:] + [residual_rows], sources[3]
    sources.append(swap_core(sources[1]))
    tiles = jnp.stack(
        [w.reshape(256, 2, 256) for w in (temporal_query, temporal_key, temporal_value)]
        + [temporal_out.reshape(2, 256, 256).swapaxes(0, 1)]
    ).transpose(2, 0, 1, 3)
    mine, theirs = (
        lax.dynamic_index_in_dim(tiles, which, axis=0, keepdims=False) for which in (c, 1 - c)
    )
    shard = after(jnp.concatenate([mine, swap_core(theirs)]), *out_own[1:])
    shards_first = [shard] + [from_first(shard, d) for d in range(1, RING)]
    parts = spatial_out_call(coords, sources, load_out(coords, out_own))

    far = [to_y(parts[2][:128], 1), to_y(parts[2][128:], -1)]
    near_p = jnp.concatenate([parts[1][:128] + far[0], parts[1][128:]])
    near_m = jnp.concatenate([parts[3][:128], parts[3][128:] + far[1]])
    first = jnp.stack(lax.optimization_barrier((*shards_first, *far))[:RING])
    first, near_p, near_m = lax.optimization_barrier((first, near_p, near_m))
    pieces = [first, from_second(first, 1), from_second(first, -1)]
    total = parts[0].astype(jnp.float32)
    for part in (to_y(near_p, 1), to_y(near_m, -1)):
        total = total + part.astype(jnp.float32)
    total = total.astype(jnp.bfloat16)
    middle, normed = norm_call(coords, residual_rows, total[:128], swap_core(total[128:]))
    normed = lax.all_to_all(
        normed.reshape(16, 8, 4096), ("z", "xh", "c"), split_axis=0, concat_axis=0, tiled=True
    ).reshape(128, 4096)
    normed, *pieces = lax.optimization_barrier((normed, *pieces))
    next_p, next_m = from_y(normed, 1), from_y(normed, -1)
    last = [from_second(pieces[1][:2], 1), from_second(pieces[2][2:], -1)]
    weights = load_temporal(coords, pieces, [(j, 0, RING) for j in (0, 1, 3)])
    *last, next_p, next_m, w_0, w_1, w_2, w_3 = lax.optimization_barrier(
        (*last, next_p, next_m, *weights)
    )
    weights = [w_0, w_1, w_2, w_3]
    weights = load_temporal(coords, last, [(2, 0, 2), (2, 2, 2)], weights)

    far = [from_y(next_p[:64], 1), from_y(next_m[64:], -1)]
    near = [next_p, next_m, swap_core(next_p), swap_core(next_m)]
    *near, own_swapped = lax.optimization_barrier((*near, swap_core(normed)))

    part_p, part_m, others = temporal_call(near, weights)
    *far, part_p, part_m, others = lax.optimization_barrier((*far, part_p, part_m, others))
    far += [swap_core(half) for half in far]
    *far, others = lax.optimization_barrier((*far, others))
    others = swap_core(others)
    part, far_others = temporal_call(far, weights)
    far_others, others = lax.optimization_barrier((far_others, others))
    part = (part.astype(jnp.float32) + swap_core(far_others).astype(jnp.float32)).astype(jnp.bfloat16)
    far = [to_y(part[:64], 1), to_y(part[64:], -1)]
    own, own_others = temporal_call([normed, own_swapped], weights)
    *far, own, own_others = lax.optimization_barrier((*far, own, own_others))
    total = own.astype(jnp.float32) + swap_core(own_others).astype(jnp.float32)
    zeros = jnp.zeros((64, 4096), jnp.bfloat16)
    for d, part, other, passed in (
        (1, part_p, others[:128], [far[0], zeros]),
        (-1, part_m, others[128:], [zeros, far[1]]),
    ):
        part = part.astype(jnp.float32) + other.astype(jnp.float32)
        part = (part + jnp.concatenate(passed).astype(jnp.float32)).astype(jnp.bfloat16)
        total = total + to_y(part, d).astype(jnp.float32)
    summed = total.astype(jnp.bfloat16).reshape(16, 8, 4096)
    summed = lax.all_to_all(summed, ("z", "xh", "c"), split_axis=0, concat_axis=0, tiled=True)
    finished = middle.astype(jnp.float32) + summed.reshape(128, 4096).astype(jnp.float32)
    return finished.astype(jnp.bfloat16).reshape(residual.shape)


def solution(mesh):
    split = Mesh(mesh.devices.reshape(SIZES), AXES)
    seq, head = ("z", "xh", "c"), ("y", "xl")
    in_specs = (
        P(head, None, seq, None),
        P(None, None, seq, head),
        P(None, None, seq, head),
        P(None, None, seq, head),
        P(head, seq),
        P(seq, head),
        P(seq, head),
        P(seq, head),
        P(head, seq),
    )
    out_specs = P(head, None, seq, None)
    return jax.shard_map(shards, mesh=split, in_specs=in_specs, out_specs=out_specs, check_vma=False)
```
